512 devices in a mesh: dp: 8 (over z), seq: 64 (over x, y, core).
Axes of the slice: x: 4, y: 8, z: 8, core: 2. Of those that a mesh axis runs over, the one named last changes fastest.
Arguments:
- inputs: bfloat16 [8, 8192, 512], P('dp', 'seq'), may hold values from -16 to 16
- weight: bfloat16 [512, 2048], P(('dp', 'seq')), may hold values from -0.25 to 0.25
- table: bfloat16 [4096, 1024], P('dp'), may hold values from -1.5 to 1.5
- grad_out: bfloat16 [8, 16384, 512], P('dp', 'seq'), may hold values from -6 to 6
- clip_speaker: int32 [8], P('dp'), may hold values from 0 to 4095
- part_speaker: int32 [8, 64], P('dp', 'seq'), may hold values from 0 to 4095
- quote_bounds: int32 [8, 64, 2], P('dp', 'seq'), may hold values from 0 to 255, as said below
Outputs:
- grad_inputs: bfloat16 [8, 8192, 512], P('dp', 'seq')
- grad_weight: float32 [512, 2048], P(('dp', 'seq'))
- grad_table: bfloat16 [4096, 1024], P('dp')
The draws below stay inside these ranges and needn't reach their ends.
Inputs may be any that keep to these rules, and one draw needn't show every extreme that they name: `quote_bounds`: each span's quoted segment is at least 32 and at most 128 frames long and lies inside the span.
All inputs are finite; a program needn't handle non-finite values.
Results may differ from the reference program's by a relative error of at most 0.0049.
Values may be sent and summed in bfloat16 or wider, within the bound.
A program may use at most 64 MiB of HBM per device.

```python
import math
import jax
import jax.numpy as jnp
import numpy as np
from jax import lax

C = 512
SPK = 4096
FILM = 1024
CLIPS = 8
SPANS = 64
IN_FRAMES = 8192
OUT_DEV = 256
OUT_FRAMES = 16384


def draw_quote_bounds(key, part):
    key = jax.random.fold_in(key, 7)
    first_key, second_key = jax.random.split(key)
    starts = jax.random.randint(first_key, (CLIPS, SPANS), 0, OUT_DEV // 2)
    lengths = jax.random.randint(second_key, (CLIPS, SPANS), OUT_DEV // 8, OUT_DEV // 2 + 1)
    starts = starts.at[0, 0].set(0)
    starts = starts.at[CLIPS - 1, SPANS - 1].set(OUT_DEV // 2 - 1)
    lengths = lengths.at[CLIPS - 1, SPANS - 1].set(OUT_DEV // 2)
    return jnp.stack([starts, starts + lengths], -1).astype(jnp.int32)


def set_ends(result, key, smallest, top_value):
    extent = result.shape
    spot = [jax.random.randint(jax.random.fold_in(key, axis), (), 0, extent[axis]) for axis in range(len(extent))]
    result = result.at[tuple(spot)].set(smallest)
    longest = extent.index(max(extent))
    spot[longest] = (spot[longest] + 1) % extent[longest]
    return result.at[tuple(spot)].set(top_value)


def with_spikes(drawn, key, source, target, shards_of, factor):
    owner, partner = [(jnp.arange(drawn.shape[dim]) // (drawn.shape[dim] // shards_of)).reshape([-1 if axis == dim else 1 for axis in range(drawn.ndim)]) for dim in (source, target)]
    chosen = jax.random.permutation(key, shards_of)[partner]
    strong = (owner == chosen) | (owner == (partner + shards_of // 2) % shards_of)
    return jnp.where(strong, factor * drawn, drawn)


def steps_of(rng, dims, pieces, low, largest):
    factor_of, own = 1.0, jax.random.fold_in(rng, 6)
    for dim, shards_of in pieces:
        steps = jnp.exp(jax.random.uniform(jax.random.fold_in(own, dim), (shards_of,), jnp.float32, low / len(pieces), largest / len(pieces)))
        factor_of = factor_of * jnp.repeat(steps, dims[dim] // shards_of).reshape([-1 if axis == dim else 1 for axis in range(len(dims))])
    return factor_of


def cumulative_ranks(count, lean):
    loads = [(1 << 20) // math.isqrt(standing ** lean) + 1 for standing in range(1, count + 1)]
    scale = 1 + sum(loads) // (1 << 30)
    return np.cumsum(np.array([max(1, weight // scale) for weight in loads]))


def ranked(own_key, shape, amount, skew):
    listing = cumulative_ranks(amount, skew)
    pick = jax.random.randint(jax.random.fold_in(own_key, 1), shape, 0, int(listing[amount - 1]))
    rank = jnp.searchsorted(jnp.asarray(listing, jnp.int32), pick, side="right")
    return jax.random.permutation(jax.random.fold_in(own_key, 2), amount)[rank].astype(jnp.int32)


def normal_values(rng, dims, deviation, reach, cuts=(), held_as=jnp.bfloat16):
    drawn = deviation * jax.random.normal(rng, dims, jnp.float32)
    if cuts:
        drawn = drawn * steps_of(rng, dims, cuts, -0.22, 0.18)
    return jnp.clip(drawn, -reach, reach).astype(held_as)


def heavy_noise(rng, shape, spread, most, shards, heavy, held_as=jnp.bfloat16):
    values = spread * jax.random.normal(rng, shape, jnp.float32)
    if shards:
        values = values * steps_of(rng, shape, shards, -0.22, 0.18)
    return jnp.clip(with_spikes(values, jax.random.fold_in(rng, 3), *heavy), -most, most).astype(held_as)


def setup_inputs(seed: int = 0) -> dict:
    keys = jax.random.split(jax.random.key(seed), 8)
    return {
        "inputs": heavy_noise(keys[0], (CLIPS, IN_FRAMES, C), 1.0, 16.0, ((0, 8), (1, 64)), (1, 2, 64, 4.0)),
        "weight": normal_values(keys[1], (C, 4 * C), C ** -0.5, 0.25, ((0, 512),)),
        "table": normal_values(keys[2], (SPK, FILM), 0.3, 1.5, ((0, 8),)),
        "grad_out": normal_values(keys[3], (CLIPS, OUT_FRAMES, C), 1.0, 6.0, ((0, 8), (1, 64))),
        "clip_speaker": set_ends(ranked(keys[4], (CLIPS,), SPK, 2), jax.random.fold_in(keys[4], 3), 0, SPK - 1).astype(jnp.int32),
        "part_speaker": set_ends(ranked(keys[5], (CLIPS, SPANS), SPK, 2), jax.random.fold_in(keys[5], 3), 0, SPK - 1).astype(jnp.int32),
        "quote_bounds": draw_quote_bounds(jax.random.fold_in(keys[7], 71), 0),
    }


def mish_grad(pre, cotangent):
    soft = jax.nn.softplus(pre)
    tangent = jnp.tanh(soft)
    return cotangent * (tangent + pre * jax.nn.sigmoid(pre) * (1.0 - tangent * tangent))

def reference(inputs, weight, table, grad_out, clip_speaker, part_speaker, quote_bounds):
    fscale = 1.0 / jnp.sqrt(jnp.float32(OUT_DEV))
    wscale = 1.0 / jnp.sqrt(jnp.float32(CLIPS * IN_FRAMES))

    def per_clip(items):
        frames_in, cotangent, speaker, parts, bounds = items
        products = jnp.dot(frames_in, weight, preferred_element_type=jnp.float32)
        zero_row = jnp.zeros((1, C), jnp.float32)
        even_out = products[:, C:2 * C] + jnp.concatenate([zero_row, products[:-1, 3 * C:]], 0)
        odd_out = products[:, 2 * C:3 * C] + jnp.concatenate([products[1:, :C], zero_row], 0)
        upsampled = jnp.stack([even_out, odd_out], 1).reshape(OUT_FRAMES, C)
        position = jnp.arange(OUT_DEV, dtype=jnp.int32)
        quoted = ((position[None, :] >= bounds[:, 0:1]) & (position[None, :] < bounds[:, 1:2])).astype(jnp.float32)
        base_row = table[speaker].astype(jnp.float32)
        part_rows = table[parts].astype(jnp.float32)
        film = (1.0 - quoted)[:, :, None] * base_row[None, None, :] + quoted[:, :, None] * part_rows[:, None, :]
        film = film.reshape(OUT_FRAMES, FILM)
        scale_part = film[:, :C]
        shift_part = film[:, C:]
        pre = upsampled * (1.0 + scale_part) + shift_part
        grad_pre = mish_grad(pre, cotangent.astype(jnp.float32))
        grad_up = (grad_pre * (1.0 + scale_part)).astype(jnp.bfloat16)
        paired = grad_up.reshape(IN_FRAMES, 2 * C)
        zero_half = jnp.zeros((1, C), jnp.bfloat16)
        odd_prev = jnp.concatenate([zero_half, paired[:-1, C:]], 0)
        even_next = jnp.concatenate([paired[1:, :C], zero_half], 0)
        taps_grad = jnp.concatenate([odd_prev, paired[:, :C], paired[:, C:], even_next], 1)
        grad_frames = lax.dot_general(taps_grad, weight, (((1,), (1,)), ((), ())), preferred_element_type=jnp.float32)
        weight_part = lax.dot_general(frames_in, taps_grad, (((0,), (0,)), ((), ())), preferred_element_type=jnp.float32)
        film_grad = (jnp.concatenate([grad_pre * upsampled, grad_pre], 1) * fscale).reshape(SPANS, OUT_DEV, FILM)
        base_sums = jnp.einsum('so,soc->sc', 1.0 - quoted, film_grad, precision=lax.Precision.HIGHEST)
        part_sums = jnp.einsum('so,soc->sc', quoted, film_grad, precision=lax.Precision.HIGHEST)
        owners = jnp.concatenate([jnp.full((SPANS,), speaker, jnp.int32), parts.astype(jnp.int32)])
        table_part = jax.ops.segment_sum(jnp.concatenate([base_sums, part_sums], 0), owners, num_segments=SPK)
        return (grad_frames.astype(jnp.bfloat16), weight_part, table_part)
    grad_inputs, weight_parts, table_parts = lax.map(per_clip, (inputs, grad_out, clip_speaker, part_speaker, quote_bounds))
    grad_weight = lax.optimization_barrier(jnp.sum(weight_parts, 0)) * wscale
    grad_table = lax.optimization_barrier(jnp.sum(table_parts, 0)).astype(jnp.bfloat16)
    return (grad_inputs, grad_weight, grad_table)
```

```python
import jax
import jax.numpy as jnp
from jax import lax
from jax.experimental import pallas as pl
from jax.experimental.pallas import tpu as pltpu
from jax.sharding import PartitionSpec as P

MESH = pl.DeviceIdType.MESH
F32 = jnp.float32
BF16 = jnp.bfloat16

NX, NY, NZ = 4, 8, 8
G = 8
C = 512
ROWS = 128
LANES = 128

(TILE, IDZ, WZ, WY, FILM, IDY, GOUT, ROWY, ROWZ, GWY, GWZ, GWX, INP, HALO, PAIR, GID, GIX, EDGE, TAB) = range(19)
CHANNELS = 19


def iota(shape, dim):
    return lax.broadcasted_iota(jnp.int32, shape, dim)


def dot(a, b):
    return jnp.dot(a, b, preferred_element_type=F32)


def dot_nt(a, b):
    return lax.dot_general(a, b, (((1,), (1,)), ((), ())), preferred_element_type=F32)


def dot_tn(a, b):
    return lax.dot_general(a, b, (((0,), (0,)), ((), ())), preferred_element_type=F32)


def mish_slope(pre):
    t = jnp.exp(-jnp.abs(pre))
    positive = pre >= 0.0
    num = jnp.where(positive, 1.0 + 2.0 * t, t * (t + 2.0))
    rest = jnp.where(positive, 2.0 * t * t, 2.0)
    inv = 1.0 / (num + rest)
    tangent = num * inv
    gate = jnp.where(positive, 1.0, t) / (1.0 + t)
    return tangent + pre * gate * (rest * (2.0 * num + rest) * inv * inv)


def kernel(
    inp, w, tab, go, clip, part, qb, o_gi, o_gw, o_gt,
    tsend, tg, idz, idy, wy, tabv, frs, frr, flm, xg, hx, xs, gov, gsend, gg, p01, wcat, pickt,
    ub, gbuf, segs, c1r, yr, zr, gws, gwr, gz, gzr, gxs, gxr, pb, gis, gir, gi2, gix, esend, ed,
    ssem, rsem, lsem,
):
    z = lax.axis_index("dp")
    s = lax.axis_index("seq")
    x = s // 16
    y = (s // 2) % NY
    c = s % 2
    m = 2 * x + c
    side = 2 * c - 1

    def at(zz, xx, yy, cc):
        return (zz, xx * 16 + yy * 2 + cc)

    def gpeer(i):
        return at(z, i // 2, y, i % 2)

    def ypeer(i):
        return at(z, x, i, c)

    def zpeer(i):
        return at(i, x, y, c)

    def xpeer(i):
        return at(z, i, y, c)

    sibling = at(z, x, y, 1 - c)

    def hpeer(i):
        return at(z, i, (y + side + NY) % NY, 1 - c)

    def remote(src, dst, chan, ss, rs, dev):
        return pltpu.make_async_remote_copy(
            src_ref=src, dst_ref=dst, send_sem=ssem.at[chan, ss], recv_sem=rsem.at[chan, rs],
            device_id=dev, device_id_type=MESH,
        )

    pending = []

    def spread(chan, me, peer, src, dst, n=8):
        def desc(d):
            i = (me + d) % n
            return remote(src(i), dst, chan, d, d, peer(i))

        @pl.loop(1, n)
        def _(d):
            desc(d).start()

        def finish():
            @pl.loop(1, n)
            def _(d):
                desc(d).wait_send()

        pending.append(finish)

    def collect(chan, me, peer, slot, n=8):
        @pl.loop(1, n)
        def _(d):
            i = (me - d + n) % n
            remote(slot(i), slot(i), chan, d, d, peer(i)).wait_recv()

    xcol = pl.multiple_of(x * LANES, LANES)
    scol = pl.multiple_of(C + x * LANES, LANES)
    get_go = pltpu.make_async_copy(go.at[0], gov, lsem.at[0])
    get_in = pltpu.make_async_copy(inp.at[0], xg.at[m], lsem.at[1])
    get_scale = pltpu.make_async_copy(tab.at[:, pl.ds(xcol, LANES)], tabv.at[:, pl.ds(0, LANES)], lsem.at[2])
    get_shift = pltpu.make_async_copy(tab.at[:, pl.ds(scol, LANES)], tabv.at[:, pl.ds(LANES, LANES)], lsem.at[3])
    for copy in (get_go, get_in, get_scale, get_shift):
        copy.start()

    barrier = pltpu.get_barrier_semaphore()

    @pl.loop(1, 8)
    def _(d):
        pl.semaphore_signal(barrier, inc=1, device_id=gpeer((m + d) % G), device_id_type=MESH)
        pl.semaphore_signal(barrier, inc=1, device_id=zpeer((z + d) % NZ), device_id_type=MESH)
        pl.semaphore_signal(barrier, inc=1, device_id=ypeer((y + d) % NY), device_id_type=MESH)

    @pl.loop(0, NX)
    def _(i):
        pl.semaphore_signal(barrier, inc=1, device_id=hpeer(i), device_id_type=MESH)

    row8 = iota((8, LANES), 0)
    lane = iota((8, LANES), 1)
    info = jnp.where(lane == 0, part[0, 0], 0)
    info = jnp.where(lane == 1, qb[0, 0, 0], info)
    info = jnp.where(lane == 2, qb[0, 0, 1], info)
    info = jnp.where(lane == 3, clip[0], info).astype(F32)
    wrow = w[...].astype(F32)
    for i in range(G):
        qi, ci = i // 2, i % 2
        taps = (1, 3) if ci == 0 else (2, 0)
        first, second = [wrow[:, k * C + qi * LANES : k * C + (qi + 1) * LANES] for k in taps]
        tsend[i] = jnp.where(row8 == 0, first, jnp.where(row8 == 1, second, info))
    tg[m] = tsend[m]

    pl.semaphore_wait(barrier, 25)

    spread(TILE, m, gpeer, lambda i: tsend.at[i], tg.at[m])
    spread(INP, x, xpeer, lambda i: inp.at[0], xg.at[m], n=NX)
    own_in = remote(inp.at[0], xg.at[m], INP, 0, 0, sibling)
    own_in.start()
    pending.append(own_in.wait_send)

    turn = (c * ((y + 1) // NY) + (1 - c) * (3 * ((NY - y) // NY))) % NX

    def halo_copy(i):
        src = inp.at[0, pl.ds(pl.multiple_of(c * 112, 16), 16), :]
        return remote(src, hx.at[(x + turn) % NX], HALO, i, (x + turn) % NX, hpeer(i))

    @pl.loop(0, NX)
    def _(i):
        halo_copy(i).start()

    def halo_sent():
        @pl.loop(0, NX)
        def _(i):
            halo_copy(i).wait_send()

    pending.append(halo_sent)

    get_go.wait()
    ri, rj = iota((256, 256), 0), iota((256, 256), 1)
    pick = jnp.where(ri < ROWS, 2 * ri, 2 * (ri - ROWS) + 1)
    gde = dot(jnp.where(rj == pick, 1.0, 0.0).astype(BF16), gov[...]).astype(BF16)
    for i in range(G):
        qi, ci = i // 2, i % 2
        gsend[i] = gde[ci * ROWS : (ci + 1) * ROWS, qi * LANES : (qi + 1) * LANES]
    gg[m] = gsend[m]
    spread(GOUT, m, gpeer, lambda i: gsend.at[i], gg.at[m])

    collect(TILE, m, gpeer, lambda i: tg.at[i])
    rows_a = jnp.zeros((8, LANES), F32)
    rows_b = rows_a
    ids = rows_a
    for i in range(G):
        tile = tg[i]
        rows_a = jnp.where(row8 == i, tile[0:1], rows_a)
        rows_b = jnp.where(row8 == i, tile[1:2], rows_b)
        ids = jnp.where(row8 == i, tile[2:3], ids)
    idz[z] = ids
    wy[y, z] = jnp.concatenate([rows_a, rows_b], 0).astype(BF16)
    spread(IDZ, z, zpeer, lambda i: idz.at[z], idz.at[z])
    spread(WZ, z, zpeer, lambda i: wy.at[y, z], wy.at[y, z])

    @pl.loop(0, 8)
    def _(b):
        row = b * LANES + iota((LANES, LANES), 0)
        tap, chan = row // C, row % C
        place = (chan // 2) % 8 * 128 + chan // 64 * 16 + tap * 8 + chan // 16 % 4 * 2 + chan % 2
        off = place - iota((LANES, LANES), 1)
        for k in range(8):
            p01[pl.ds(pl.multiple_of(b * LANES, LANES), LANES), k * LANES : (k + 1) * LANES] = jnp.where(
                off == k * LANES, 1.0, 0.0
            ).astype(BF16)

    collect(WZ, z, zpeer, lambda i: wy.at[y, i])
    spread(WY, y, ypeer, lambda i: wy.at[y], wy.at[y])

    collect(IDZ, z, zpeer, lambda i: idz.at[i])
    base = (z * C).astype(F32)
    lane512 = iota((8, C), 1).astype(F32)
    packed = jnp.zeros((8, LANES), F32)
    asked = []
    for i in range(NZ):
        tile = idz[i]
        part_id, clip_id = tile[:, 0:1], tile[:, 3:4]
        asked.append(jnp.where(part_id - base == lane512, 1.0, 0.0))
        asked.append(jnp.where(clip_id - base == lane512, 1.0, 0.0))
        packed = jnp.where(lane == i, part_id, jnp.where(lane == 8 + i, clip_id, packed))
    idy[y] = packed
    spread(IDY, y, ypeer, lambda i: idy.at[y], idy.at[y])
    get_scale.wait()
    get_shift.wait()
    served = dot(jnp.concatenate(asked, 0).astype(BF16), tabv[...]).astype(BF16)
    for i in range(NZ):
        frs[i] = served[16 * i : 16 * (i + 1)]
    frr[z] = frs[z]
    spread(FILM, z, zpeer, lambda i: frs.at[i], frr.at[z])

    def hand_on(d):
        i = (x - d + NX) % NX
        return remote(xg.at[2 * i + c], xg.at[2 * i + c], INP, 4 + d, 4 + d, sibling)

    @pl.loop(1, NX)
    def _(d):
        i = (x - d + NX) % NX
        remote(xg.at[2 * i + c], xg.at[2 * i + c], INP, d, d, xpeer(i)).wait_recv()
        hand_on(d).start()

    def handed_on():
        @pl.loop(1, NX)
        def _(d):
            hand_on(d).wait_send()

    pending.append(handed_on)

    get_in.wait()
    remote(xg.at[2 * x + 1 - c], xg.at[2 * x + 1 - c], INP, 0, 0, sibling).wait_recv()

    @pl.loop(1, NX)
    def _(d):
        i = (x - d + NX) % NX
        remote(xg.at[2 * i + 1 - c], xg.at[2 * i + 1 - c], INP, 4 + d, 4 + d, sibling).wait_recv()

    @pl.loop(0, NX)
    def _(i):
        remote(hx.at[i], hx.at[i], HALO, i, i, hpeer(i)).wait_recv()

    shift = jnp.where(rj - ri == side, 1.0, 0.0).astype(BF16)
    rowp = iota((256, C), 0)
    for i in range(NX):
        pair = xg[2 * i : 2 * i + 2].reshape(256, C)
        block = hx[i].astype(F32)
        outer = jnp.where(c == 0, block[15:16], block[0:1])
        inside = i * 16 + y * 2 + c != c * 63
        outer = jnp.where(inside, outer, 0.0)
        moved = jnp.where(rowp == c * 255, outer, dot(shift, pair))
        xs[256 * i : 256 * (i + 1)] = moved.astype(BF16)

    collect(IDY, y, ypeer, lambda i: idy.at[i])
    for i in range(NZ):
        for k in range(NY):
            match = jnp.where(idy[k][:, i : i + 1] - base == lane512, 1.0, 0.0)
            if k % 2 == 0:
                even = match
            else:
                pickt[80 * i + 8 * (k - 1) : 80 * i + 8 * (k + 1)] = jnp.concatenate([even, match], 0).astype(BF16)
        match = jnp.where(idy[0][:, 8 + i : 9 + i] - base == lane512, 1.0, 0.0)
        pickt[80 * i + 64 : 80 * i + 80] = jnp.concatenate([match, match], 0).astype(BF16)

    collect(FILM, z, zpeer, lambda i: frr.at[i])
    film = frr[0].astype(F32)
    for i in range(1, NZ):
        film = film + frr[i].astype(F32)
    flm[...] = film
    collect(GOUT, m, gpeer, lambda i: gg.at[i])
    collect(WY, y, ypeer, lambda i: wy.at[i])

    wcat[...] = dot(p01[...], wy[...].reshape(2 * C, LANES)).astype(BF16)
    frames = xg[...].reshape(2 * C, C)
    ub[...] = dot(frames, wcat[0:C]) + dot(xs[...], wcat[C : 2 * C])

    base_row = flm[8:9]
    frame = (2 * iota((ROWS, LANES), 0) + c).astype(F32)
    part_scale = jnp.zeros((8, LANES), F32)
    part_shift = part_scale
    base_scale = jnp.zeros((1, LANES), F32)
    base_shift = base_scale
    for i in range(G):
        u = ub[ROWS * i : ROWS * (i + 1)]
        bounds = tg[i]
        quoted = (frame >= bounds[2:3, 1:2]) & (frame < bounds[2:3, 2:3])
        scale = jnp.where(quoted, flm[i : i + 1, 0:LANES], base_row[:, 0:LANES])
        offset = jnp.where(quoted, flm[i : i + 1, LANES:], base_row[:, LANES:])
        gain = 1.0 + scale
        grad = gg[i].astype(F32) * mish_slope(u * gain + offset)
        gbuf[ROWS * i : ROWS * (i + 1)] = (grad * gain).astype(BF16)
        gu = grad * u
        part_scale = jnp.where(row8 == i, jnp.sum(jnp.where(quoted, gu, 0.0), 0, keepdims=True), part_scale)
        part_shift = jnp.where(row8 == i, jnp.sum(jnp.where(quoted, grad, 0.0), 0, keepdims=True), part_shift)
        base_scale = base_scale + jnp.sum(jnp.where(quoted, 0.0, gu), 0, keepdims=True)
        base_shift = base_shift + jnp.sum(jnp.where(quoted, 0.0, grad), 0, keepdims=True)
    fscale = 1.0 / 16.0
    segs[0] = jnp.concatenate([part_scale, jnp.where(row8 == 0, base_scale, 0.0)], 0) * fscale
    segs[1] = jnp.concatenate([part_shift, jnp.where(row8 == 0, base_shift, 0.0)], 0) * fscale
    pair_copy = remote(segs.at[1 - c], c1r, PAIR, 0, 0, sibling)
    pair_copy.start()

    gall = gbuf[...]
    gw0 = dot_tn(gall, frames).astype(BF16)
    gw1 = dot_tn(gall, xs[...]).astype(BF16)
    gwp = (dot(gw0, p01[0:C]) + dot(gw1, p01[C : 2 * C])).astype(BF16)
    for i in range(NY):
        gws[i] = gwp[:, LANES * i : LANES * (i + 1)]
    gwr[y] = gws[y]
    spread(GWY, y, ypeer, lambda i: gws.at[i], gwr.at[y])

    back = jnp.where(ri - rj == side, 1.0, 0.0).astype(BF16)
    edges = jnp.zeros((8, LANES), F32)
    for i in range(NX):
        pair = gbuf[256 * i : 256 * (i + 1)]
        moved = dot(back, pair).astype(BF16)
        grads = dot_nt(pair, wcat[0:C]) + dot_nt(moved, wcat[C : 2 * C])
        pb[2 * i] = grads[0:ROWS]
        pb[2 * i + 1] = grads[ROWS:]
        gis[i] = pb[2 * i + 1 - c].astype(BF16)
        remote(gis.at[i], gir.at[i], GID, i, i, sibling).start()
        outer = jnp.where(c == 0, pair[0:16].astype(F32)[0:1], pair[240:256].astype(F32)[15:16])
        edges = jnp.where(row8 == i, outer, edges)
    edge_rows = dot_nt(edges.astype(BF16), wcat[C : 2 * C])

    def edge_copy(i):
        return remote(esend.at[i], ed.at[x], EDGE, i, x, hpeer((i + turn) % NX))

    for i in range(NX):
        esend[i] = jnp.broadcast_to(edge_rows[i : i + 1], (8, C))

    @pl.loop(0, NX)
    def _(i):
        edge_copy(i).start()

    pair_copy.wait_recv()
    yr[y] = segs[c] + c1r[...]
    spread(ROWY, y, ypeer, lambda i: yr.at[y], yr.at[y])

    for i in range(NX):
        remote(gis.at[i], gir.at[i], GID, i, i, sibling).wait_recv()
        total = pb[2 * i + c] + gir[i].astype(F32)
        pb[2 * i + c] = total
        gi2[i] = total.astype(BF16)
    spread(GIX, x, xpeer, lambda i: gi2.at[i], gix.at[x], n=NX)

    collect(ROWY, y, ypeer, lambda i: yr.at[i])
    sums = yr[0, 8:16]
    for i in range(1, NY):
        sums = sums + yr[i, 8:16]
    pieces = [yr[i, 0:8] for i in range(NY)] + [sums, jnp.zeros((8, LANES), F32)]
    zr[z] = jnp.concatenate(pieces, 0).astype(BF16)
    spread(ROWZ, z, zpeer, lambda i: zr.at[z], zr.at[z])

    collect(GWY, y, ypeer, lambda i: gwr.at[i])
    gsum = gwr[0].astype(F32)
    for i in range(1, NY):
        gsum = gsum + gwr[i].astype(F32)
    turned = gsum.T
    for i in range(NZ):
        gz[i] = turned[16 * i : 16 * (i + 1)]
    gzr[z] = gz[z]
    spread(GWZ, z, zpeer, lambda i: gz.at[i], gzr.at[z])

    ocol = pl.multiple_of(c * C + x * LANES, LANES)
    collect(ROWZ, z, zpeer, lambda i: zr.at[i])
    o_gt[:, pl.ds(ocol, LANES)] = dot_tn(pickt[...], zr[...].reshape(640, LANES)).astype(BF16)
    mine = o_gt.at[:, pl.ds(ocol, LANES)]
    spread(TAB, x, xpeer, lambda i: mine, mine, n=NX)
    own_tab = remote(mine, mine, TAB, 0, 0, sibling)
    own_tab.start()
    pending.append(own_tab.wait_send)

    collect(GWZ, z, zpeer, lambda i: gzr.at[i])
    gsum = gzr[0]
    for i in range(1, NZ):
        gsum = gsum + gzr[i]
    gsum = gsum * (1.0 / 256.0)
    for i in range(G):
        gxs[i] = jnp.where(row8 == 0, gsum[i : i + 1], gsum[8 + i : 9 + i])
    gxr[m] = gxs[m]
    spread(GWX, m, gpeer, lambda i: gxs.at[i], gxr.at[m])

    collect(GIX, x, xpeer, lambda i: gix.at[i], n=NX)

    @pl.loop(0, NX)
    def _(i):
        remote(ed.at[i], ed.at[i], EDGE, i, i, hpeer(i)).wait_recv()

    gix[x] = jnp.zeros((ROWS, C), BF16)
    total = pb[2 * x + c]
    edge = ed[0, 0:1]
    for i in range(NX):
        total = total + gix[i].astype(F32)
        if i:
            edge = edge + ed[i, 0:1]
    edge = jnp.where(s != c * 63, edge, 0.0)
    total = total + jnp.where(iota((ROWS, C), 0) == c * 127, edge, 0.0)
    o_gi[0] = total.astype(BF16)

    collect(GWX, m, gpeer, lambda i: gxr.at[i])
    for i in range(G):
        qi, ci = i // 2, i % 2
        taps = (1, 3) if ci == 0 else (2, 0)
        for t, k in enumerate(taps):
            o_gw[:, k * C + qi * LANES : k * C + (qi + 1) * LANES] = gxr[i, t : t + 1]

    def column(i, cc):
        return o_gt.at[:, pl.ds(pl.multiple_of(cc * C + i * LANES, LANES), LANES)]

    def pass_on(d):
        i = (x - d + NX) % NX
        return remote(column(i, c), column(i, c), TAB, 4 + d, 4 + d, sibling)

    @pl.loop(1, NX)
    def _(d):
        i = (x - d + NX) % NX
        remote(column(i, c), column(i, c), TAB, d, d, xpeer(i)).wait_recv()
        pass_on(d).start()

    remote(column(x, 1 - c), column(x, 1 - c), TAB, 0, 0, sibling).wait_recv()

    @pl.loop(1, NX)
    def _(d):
        i = (x - d + NX) % NX
        remote(column(i, 1 - c), column(i, 1 - c), TAB, 4 + d, 4 + d, sibling).wait_recv()

    pair_copy.wait_send()
    for i in range(NX):
        remote(gis.at[i], gir.at[i], GID, i, i, sibling).wait_send()

    @pl.loop(0, NX)
    def _(i):
        edge_copy(i).wait_send()

    @pl.loop(1, NX)
    def _(d):
        pass_on(d).wait_send()

    for finish in pending:
        finish()


def body(inputs, weight, table, grad_out, clip_speaker, part_speaker, quote_bounds):
    vmem = pl.BlockSpec(memory_space=pltpu.VMEM)
    smem = pl.BlockSpec(memory_space=pltpu.SMEM)
    hbm = pl.BlockSpec(memory_space=pl.ANY)
    V = pltpu.VMEM
    return pl.pallas_call(
        kernel,
        out_shape=(
            jax.ShapeDtypeStruct(inputs.shape, BF16),
            jax.ShapeDtypeStruct(weight.shape, F32),
            jax.ShapeDtypeStruct(table.shape, BF16),
        ),
        in_specs=[hbm, vmem, hbm, hbm, smem, smem, smem],
        out_specs=(vmem, vmem, vmem),
        scratch_shapes=[
            V((G, 8, LANES), F32),
            V((G, 8, LANES), F32),
            V((NZ, 8, LANES), F32),
            V((NY, 8, LANES), F32),
            V((NY, NZ, 16, LANES), BF16),
            V((C, 2 * LANES), BF16),
            V((NZ, 16, 2 * LANES), BF16),
            V((NZ, 16, 2 * LANES), BF16),
            V((16, 2 * LANES), F32),
            V((G, ROWS, C), BF16),
            V((NX, 16, C), BF16),
            V((G * ROWS, C), BF16),
            V((2 * ROWS, C), BF16),
            V((G, ROWS, LANES), BF16),
            V((G, ROWS, LANES), BF16),
            V((2 * C, 2 * C), BF16),
            V((2 * C, LANES), BF16),
            V((640, C), BF16),
            V((G * ROWS, LANES), F32),
            V((G * ROWS, LANES), BF16),
            V((2, 16, LANES), F32),
            V((16, LANES), F32),
            V((NY, 16, LANES), F32),
            V((NZ, 80, LANES), BF16),
            V((NY, LANES, LANES), BF16),
            V((NY, LANES, LANES), BF16),
            V((NZ, 16, LANES), F32),
            V((NZ, 16, LANES), F32),
            V((G, 8, LANES), F32),
            V((G, 8, LANES), F32),
            V((G, ROWS, C), F32),
            V((NX, ROWS, C), BF16),
            V((NX, ROWS, C), BF16),
            V((NX, ROWS, C), BF16),
            V((NX, ROWS, C), BF16),
            V((NX, 8, C), F32),
            V((NX, 8, C), F32),
            pltpu.SemaphoreType.DMA((CHANNELS, 8)),
            pltpu.SemaphoreType.DMA((CHANNELS, 8)),
            pltpu.SemaphoreType.DMA((4,)),
        ],
        compiler_params=pltpu.CompilerParams(
            collective_id=0, has_side_effects=True, vmem_limit_bytes=48 * 1024 * 1024
        ),
        cost_estimate=pl.CostEstimate(flops=2_000_000_000, bytes_accessed=8_000_000, transcendentals=131072),
    )(inputs, weight, table, grad_out, clip_speaker, part_speaker, quote_bounds)


def solution(mesh):
    placed = (
        P("dp", "seq", None),
        P(("dp", "seq"), None),
        P("dp", None),
        P("dp", "seq", None),
        P("dp"),
        P("dp", "seq"),
        P("dp", "seq", None),
    )
    return jax.shard_map(
        body,
        mesh=mesh,
        in_specs=placed,
        out_specs=(P("dp", "seq", None), P(("dp", "seq"), None), P("dp", None)),
        check_vma=False,
    )
```

```python
import jax
import jax.numpy as jnp
from jax import lax
from jax.experimental import pallas as pl
from jax.experimental.pallas import tpu as pltpu
from jax.sharding import PartitionSpec as P

MESH = pl.DeviceIdType.MESH
F32 = jnp.float32
BF16 = jnp.bfloat16

NX, NY, NZ = 4, 8, 8
G = 8
C = 512
ROWS = 128
LANES = 128

(TILE, IDZ, WZ, WY, FILM, IDY, GOUT, ROWY, ROWZ, GWY, GWZ, GWX, HALO, PAIR, GID, GIX, EDGE) = range(17)
INP, TAB = 17, 22
CHANNELS = 27


def iota(shape, dim):
    return lax.broadcasted_iota(jnp.int32, shape, dim)


def dot(a, b):
    return jnp.dot(a, b, preferred_element_type=F32)


def dot_nt(a, b):
    return lax.dot_general(a, b, (((1,), (1,)), ((), ())), preferred_element_type=F32)


def dot_tn(a, b):
    return lax.dot_general(a, b, (((0,), (0,)), ((), ())), preferred_element_type=F32)


def mish_slope(pre):
    t = jnp.exp(-jnp.abs(pre))
    positive = pre >= 0.0
    num = jnp.where(positive, 1.0 + 2.0 * t, t * (t + 2.0))
    rest = jnp.where(positive, 2.0 * t * t, 2.0)
    inv = 1.0 / (num + rest)
    tangent = num * inv
    gate = jnp.where(positive, 1.0, t) / (1.0 + t)
    return tangent + pre * gate * (rest * (2.0 * num + rest) * inv * inv)


def kernel(
    inp, whbm, tab, go, clip, part, qb, o_gi, o_gw, o_gt, w,
    tsend, tg, idz, idy, wy, tabv, frs, frr, flm, xg, hx, xx, gov, gsend, gg, p01, wcat, pickt,
    gbuf, segs, c1r, yr, zr, gws, gwr, gz, gzr, gxs, gxr, pb, gis, gir, gi2, gix, esend, ed,
    ssem, rsem, lsem,
):
    z = lax.axis_index("dp")
    s = lax.axis_index("seq")
    x = s // 16
    y = (s // 2) % NY
    c = s % 2
    m = 2 * x + c
    side = 2 * c - 1

    def at(zz, xx, yy, cc):
        return (zz, xx * 16 + yy * 2 + cc)

    def gpeer(i):
        return at(z, i // 2, y, i % 2)

    def ypeer(i):
        return at(z, x, i, c)

    def zpeer(i):
        return at(i, x, y, c)

    def xpeer(i):
        return at(z, i, y, c)

    sibling = at(z, x, y, 1 - c)

    def hpeer(i):
        return at(z, i, (y + side + NY) % NY, 1 - c)

    def remote(src, dst, send, recv, dev):
        return pltpu.make_async_remote_copy(
            src_ref=src, dst_ref=dst, send_sem=ssem.at[send], recv_sem=rsem.at[recv],
            device_id=dev, device_id_type=MESH,
        )

    pending = []
    waiting = {}

    def watch(chan, ref):
        whole = remote(ref, ref, chan, chan, sibling)
        pending.append(whole.wait_send)
        waiting[chan] = whole.wait_recv

    def spread(chan, me, peer, src, slot, whole, n=8):
        @pl.loop(1, n)
        def _(d):
            i = (me + d) % n
            remote(src(i), slot(me), chan, chan, peer(i)).start()

        watch(chan, whole)

    def collect(chan):
        waiting.pop(chan)()

    def x_spread(base, src, slot, slots):
        @pl.loop(1, NX)
        def _(d):
            remote(src, slot(x, c), base, base + d, xpeer((x + d) % NX)).start()

        remote(src, slot(x, c), base, base, sibling).start()
        pending.append(remote(slots(4), slots(4), base, base, sibling).wait_send)
        waiting[base] = remote(slot(x, 1 - c), slot(x, 1 - c), base, base, sibling).wait_recv
        for d in range(1, NX):
            mine = slot((x - d + NX) % NX, c)
            waiting[base + d] = remote(mine, mine, base, base + d, sibling).wait_recv

    def x_hand_on(base, slot, slots):
        for d in range(1, NX):
            collect(base + d)
            mine = slot((x - d + NX) % NX, c)
            remote(mine, mine, base + 4, base + 4, sibling).start()

        watch(base + 4, slots(3))

    def column(i, cc):
        return o_gt.at[:, pl.ds(pl.multiple_of(cc * C + i * LANES, LANES), LANES)]

    def columns(n):
        return o_gt.at[:, pl.ds(0, n * LANES)]

    barrier = pltpu.get_barrier_semaphore()

    @pl.loop(1, 8)
    def _(d):
        pl.semaphore_signal(barrier, inc=1, device_id=gpeer((m + d) % G), device_id_type=MESH)
        pl.semaphore_signal(barrier, inc=1, device_id=zpeer((z + d) % NZ), device_id_type=MESH)
        pl.semaphore_signal(barrier, inc=1, device_id=ypeer((y + d) % NY), device_id_type=MESH)

    @pl.loop(0, NX)
    def _(i):
        pl.semaphore_signal(barrier, inc=1, device_id=hpeer(i), device_id_type=MESH)

    xcol = pl.multiple_of(x * LANES, LANES)
    scol = pl.multiple_of(C + x * LANES, LANES)
    get_go = pltpu.make_async_copy(go.at[0], gov, lsem.at[0])
    get_in = pltpu.make_async_copy(inp.at[0], xg.at[m], lsem.at[1])
    get_scale = pltpu.make_async_copy(tab.at[:, pl.ds(xcol, LANES)], tabv.at[:, pl.ds(0, LANES)], lsem.at[2])
    get_shift = pltpu.make_async_copy(tab.at[:, pl.ds(scol, LANES)], tabv.at[:, pl.ds(LANES, LANES)], lsem.at[3])
    get_w = pltpu.make_async_copy(whbm, w, lsem.at[4])
    for copy in (get_w, get_go, get_in, get_scale, get_shift):
        copy.start()

    row8 = iota((8, LANES), 0)
    lane = iota((8, LANES), 1)
    info = jnp.where(lane == 0, part[0, 0], 0)
    info = jnp.where(lane == 1, qb[0, 0, 0], info)
    info = jnp.where(lane == 2, qb[0, 0, 1], info)
    info = jnp.where(lane == 3, clip[0], info).astype(F32)
    get_w.wait()
    wrow = w[...].astype(F32)
    for i in range(G):
        qi, ci = i // 2, i % 2
        taps = (1, 3) if ci == 0 else (2, 0)
        first, second = [wrow[:, k * C + qi * LANES : k * C + (qi + 1) * LANES] for k in taps]
        tsend[i] = jnp.where(row8 == 0, first, jnp.where(row8 == 1, second, info))
    tg[m] = tsend[m]

    pl.semaphore_wait(barrier, 25)

    spread(TILE, m, gpeer, lambda i: tsend.at[i], lambda i: tg.at[i], tg.at[pl.ds(0, 7)])

    def frame_slot(i, cc):
        return xg.at[2 * i + cc]

    def frame_slots(n):
        return xg.at[pl.ds(0, n)]

    x_spread(INP, inp.at[0], frame_slot, frame_slots)
    turn = (c * ((y + 1) // NY) + (1 - c) * (3 * ((NY - y) // NY))) % NX

    @pl.loop(0, NX)
    def _(i):
        src = inp.at[0, pl.ds(pl.multiple_of(c * 112, 16), 16), :]
        remote(src, hx.at[(x + turn) % NX], HALO, HALO, hpeer(i)).start()

    watch(HALO, hx)

    get_go.wait()
    ri, rj = iota((256, 256), 0), iota((256, 256), 1)
    pick = jnp.where(ri < ROWS, 2 * ri, 2 * (ri - ROWS) + 1)
    gde = dot(jnp.where(rj == pick, 1.0, 0.0).astype(BF16), gov[...]).astype(BF16)
    for i in range(G):
        qi, ci = i // 2, i % 2
        gsend[i] = gde[ci * ROWS : (ci + 1) * ROWS, qi * LANES : (qi + 1) * LANES]
    gg[m] = gsend[m]
    spread(GOUT, m, gpeer, lambda i: gsend.at[i], lambda i: gg.at[i], gg.at[pl.ds(0, 7)])

    collect(TILE)
    rows_a = jnp.zeros((8, LANES), F32)
    rows_b = rows_a
    ids = rows_a
    for i in range(G):
        tile = tg[i]
        rows_a = jnp.where(row8 == i, tile[0:1], rows_a)
        rows_b = jnp.where(row8 == i, tile[1:2], rows_b)
        ids = jnp.where(row8 == i, tile[2:3], ids)
    idz[z] = ids
    wy[y, z] = jnp.concatenate([rows_a, rows_b], 0).astype(BF16)
    spread(IDZ, z, zpeer, lambda i: idz.at[z], lambda i: idz.at[i], idz.at[pl.ds(0, 7)])
    spread(WZ, z, zpeer, lambda i: wy.at[y, z], lambda i: wy.at[y, i], wy.at[y, pl.ds(0, 7)])

    @pl.loop(0, 8)
    def _(b):
        row = b * LANES + iota((LANES, LANES), 0)
        tap, chan = row // C, row % C
        place = (chan // 2) % 8 * 128 + chan // 64 * 16 + tap * 8 + chan // 16 % 4 * 2 + chan % 2
        off = place - iota((LANES, LANES), 1)
        for k in range(8):
            p01[pl.ds(pl.multiple_of(b * LANES, LANES), LANES), k * LANES : (k + 1) * LANES] = jnp.where(
                off == k * LANES, 1.0, 0.0
            ).astype(BF16)

    collect(WZ)
    spread(WY, y, ypeer, lambda i: wy.at[y], lambda i: wy.at[i], wy.at[pl.ds(0, 7)])

    collect(IDZ)
    base = (z * C).astype(F32)
    lane512 = iota((8, C), 1).astype(F32)
    packed = jnp.zeros((8, LANES), F32)
    asked = []
    for i in range(NZ):
        tile = idz[i]
        part_id, clip_id = tile[:, 0:1], tile[:, 3:4]
        asked.append(jnp.where(part_id - base == lane512, 1.0, 0.0))
        asked.append(jnp.where(clip_id - base == lane512, 1.0, 0.0))
        packed = jnp.where(lane == i, part_id, jnp.where(lane == 8 + i, clip_id, packed))
    idy[y] = packed
    spread(IDY, y, ypeer, lambda i: idy.at[y], lambda i: idy.at[i], idy.at[pl.ds(0, 7)])
    get_scale.wait()
    get_shift.wait()
    served = dot(jnp.concatenate(asked, 0).astype(BF16), tabv[...]).astype(BF16)
    for i in range(NZ):
        frs[i] = served[16 * i : 16 * (i + 1)]
    frr[z] = frs[z]
    spread(FILM, z, zpeer, lambda i: frs.at[i], lambda i: frr.at[i], frr.at[pl.ds(0, 7)])

    x_hand_on(INP, frame_slot, frame_slots)
    get_in.wait()
    collect(INP)
    collect(INP + 4)
    collect(HALO)

    shift = jnp.where(rj - ri == side, 1.0, 0.0).astype(BF16)
    rowp = iota((256, C), 0)
    for i in range(NX):
        pair = xg[2 * i : 2 * i + 2].reshape(256, C)
        block = hx[i].astype(F32)
        outer = jnp.where(c == 0, block[15:16], block[0:1])
        inside = i * 16 + y * 2 + c != c * 63
        outer = jnp.where(inside, outer, 0.0)
        moved = jnp.where(rowp == c * 255, outer, dot(shift, pair))
        xx[256 * i : 256 * (i + 1)] = (dot(pair, p01[0:C]) + dot(moved.astype(BF16), p01[C : 2 * C])).astype(BF16)

    collect(FILM)
    film = frr[0].astype(F32)
    for i in range(1, NZ):
        film = film + frr[i].astype(F32)
    flm[...] = film
    collect(GOUT)
    collect(WY)

    arrived = wy[...].reshape(2 * C, LANES)
    base_row = flm[8:9]
    frame = (2 * iota((ROWS, LANES), 0) + c).astype(F32)
    part_scale = jnp.zeros((8, LANES), F32)
    part_shift = part_scale
    base_scale = jnp.zeros((1, LANES), F32)
    base_shift = base_scale
    for i in range(G):
        if i % 2 == 0:
            u_pair = dot(xx[ROWS * i : ROWS * (i + 2)], arrived)
        u = u_pair[ROWS * (i % 2) : ROWS * (i % 2 + 1)]
        bounds = tg[i]
        quoted = (frame >= bounds[2:3, 1:2]) & (frame < bounds[2:3, 2:3])
        scale = jnp.where(quoted, flm[i : i + 1, 0:LANES], base_row[:, 0:LANES])
        offset = jnp.where(quoted, flm[i : i + 1, LANES:], base_row[:, LANES:])
        gain = 1.0 + scale
        grad = gg[i].astype(F32) * mish_slope(u * gain + offset)
        gbuf[ROWS * i : ROWS * (i + 1)] = (grad * gain).astype(BF16)
        gu = grad * u
        part_scale = jnp.where(row8 == i, jnp.sum(jnp.where(quoted, gu, 0.0), 0, keepdims=True), part_scale)
        part_shift = jnp.where(row8 == i, jnp.sum(jnp.where(quoted, grad, 0.0), 0, keepdims=True), part_shift)
        base_scale = base_scale + jnp.sum(jnp.where(quoted, 0.0, gu), 0, keepdims=True)
        base_shift = base_shift + jnp.sum(jnp.where(quoted, 0.0, grad), 0, keepdims=True)
    fscale = 1.0 / 16.0
    segs[0] = jnp.concatenate([part_scale, jnp.where(row8 == 0, base_scale, 0.0)], 0) * fscale
    segs[1] = jnp.concatenate([part_shift, jnp.where(row8 == 0, base_shift, 0.0)], 0) * fscale
    remote(segs.at[1 - c], c1r, PAIR, PAIR, sibling).start()
    watch(PAIR, c1r)

    gwp = dot_tn(gbuf[...], xx[...]).astype(BF16)
    for i in range(NY):
        gws[i] = gwp[:, LANES * i : LANES * (i + 1)]

    collect(PAIR)
    yr[y] = segs[c] + c1r[...]
    spread(ROWY, y, ypeer, lambda i: yr.at[y], lambda i: yr.at[i], yr.at[pl.ds(0, 7)])
    gwr[y] = gws[y]
    spread(GWY, y, ypeer, lambda i: gws.at[i], lambda i: gwr.at[i], gwr.at[pl.ds(0, 7)])

    wcat[...] = dot(p01[...], arrived).astype(BF16)
    back = jnp.where(ri - rj == side, 1.0, 0.0).astype(BF16)
    edges = jnp.zeros((8, LANES), F32)
    for i in range(NX):
        pair = gbuf[256 * i : 256 * (i + 1)]
        moved = dot(back, pair).astype(BF16)
        grads = dot_nt(pair, wcat[0:C]) + dot_nt(moved, wcat[C : 2 * C])
        pb[2 * i] = grads[0:ROWS]
        pb[2 * i + 1] = grads[ROWS:]
        gis[i] = pb[2 * i + 1 - c].astype(BF16)
        remote(gis.at[i], gir.at[i], GID, GID, sibling).start()
        outer = jnp.where(c == 0, pair[0:16].astype(F32)[0:1], pair[240:256].astype(F32)[15:16])
        edges = jnp.where(row8 == i, outer, edges)
    watch(GID, gir)
    edge_rows = dot_nt(edges.astype(BF16), wcat[C : 2 * C])

    for i in range(NX):
        esend[i] = jnp.broadcast_to(edge_rows[i : i + 1], (8, C))

    @pl.loop(0, NX)
    def _(i):
        remote(esend.at[i], ed.at[x], EDGE, EDGE, hpeer((i + turn) % NX)).start()

    watch(EDGE, ed)
    collect(IDY)
    for i in range(NZ):
        for k in range(NY):
            match = jnp.where(idy[k][:, i : i + 1] - base == lane512, 1.0, 0.0)
            if k % 2 == 0:
                even = match
            else:
                pickt[80 * i + 8 * (k - 1) : 80 * i + 8 * (k + 1)] = jnp.concatenate([even, match], 0).astype(BF16)
        match = jnp.where(idy[0][:, 8 + i : 9 + i] - base == lane512, 1.0, 0.0)
        pickt[80 * i + 64 : 80 * i + 80] = jnp.concatenate([match, match], 0).astype(BF16)

    collect(ROWY)
    sums = yr[0, 8:16]
    for i in range(1, NY):
        sums = sums + yr[i, 8:16]
    pieces = [yr[i, 0:8] for i in range(NY)] + [sums, jnp.zeros((8, LANES), F32)]
    zr[z] = jnp.concatenate(pieces, 0).astype(BF16)
    spread(ROWZ, z, zpeer, lambda i: zr.at[z], lambda i: zr.at[i], zr.at[pl.ds(0, 7)])

    collect(GID)
    for i in range(NX):
        total = pb[2 * i + c] + gir[i].astype(F32)
        pb[2 * i + c] = total
        gi2[i] = total.astype(BF16)
    spread(GIX, x, xpeer, lambda i: gi2.at[i], lambda i: gix.at[i], gix.at[pl.ds(0, 3)], n=NX)

    collect(GWY)
    gsum = gwr[0].astype(F32)
    for i in range(1, NY):
        gsum = gsum + gwr[i].astype(F32)
    turned = gsum.T
    for i in range(NZ):
        gz[i] = turned[16 * i : 16 * (i + 1)]
    gzr[z] = gz[z]
    spread(GWZ, z, zpeer, lambda i: gz.at[i], lambda i: gzr.at[i], gzr.at[pl.ds(0, 7)])

    ocol = pl.multiple_of(c * C + x * LANES, LANES)
    collect(ROWZ)
    o_gt[:, pl.ds(ocol, LANES)] = dot_tn(pickt[...], zr[...].reshape(640, LANES)).astype(BF16)
    x_spread(TAB, column(x, c), column, columns)

    collect(GWZ)
    gsum = gzr[0]
    for i in range(1, NZ):
        gsum = gsum + gzr[i]
    gsum = gsum * (1.0 / 256.0)
    for i in range(G):
        gxs[i] = jnp.where(row8 == 0, gsum[i : i + 1], gsum[8 + i : 9 + i])
    gxr[m] = gxs[m]
    spread(GWX, m, gpeer, lambda i: gxs.at[i], lambda i: gxr.at[i], gxr.at[pl.ds(0, 7)])

    collect(GIX)
    collect(EDGE)
    gix[x] = jnp.zeros((ROWS, C), BF16)
    total = pb[2 * x + c]
    edge = ed[0, 0:1]
    for i in range(NX):
        total = total + gix[i].astype(F32)
        if i:
            edge = edge + ed[i, 0:1]
    edge = jnp.where(s != c * 63, edge, 0.0)
    total = total + jnp.where(iota((ROWS, C), 0) == c * 127, edge, 0.0)
    o_gi[0] = total.astype(BF16)

    x_hand_on(TAB, column, columns)
    collect(GWX)
    for i in range(G):
        qi, ci = i // 2, i % 2
        taps = (1, 3) if ci == 0 else (2, 0)
        for t, k in enumerate(taps):
            o_gw[:, k * C + qi * LANES : k * C + (qi + 1) * LANES] = gxr[i, t : t + 1]
    collect(TAB)
    collect(TAB + 4)

    for finish in pending:
        finish()


def place(gi, gw, gt, o_gi, o_gw, o_gt, sem):
    copies = [pltpu.make_async_copy(a, b, sem.at[k]) for k, (a, b) in enumerate(((gt, o_gt), (gi, o_gi), (gw, o_gw)))]
    for copy in copies:
        copy.start()
    for copy in copies:
        copy.wait()


def body(inputs, weight, table, grad_out, clip_speaker, part_speaker, quote_bounds):
    vmem = pl.BlockSpec(memory_space=pltpu.VMEM)
    hbm = pl.BlockSpec(memory_space=pltpu.HBM)
    smem = pl.BlockSpec(memory_space=pltpu.SMEM)
    V = pltpu.VMEM
    large = [pltpu.with_memory_space_constraint(a, pltpu.HBM) for a in (inputs, weight, table, grad_out)]
    outs = pl.pallas_call(
        kernel,
        out_shape=(
            jax.ShapeDtypeStruct(inputs.shape, BF16),
            jax.ShapeDtypeStruct(weight.shape, F32),
            jax.ShapeDtypeStruct(table.shape, BF16),
        ),
        in_specs=[hbm] * 4 + [smem] * 3,
        out_specs=(vmem, vmem, vmem),
        scratch_shapes=[
            V((1, 4 * C), BF16),
            V((G, 8, LANES), F32),
            V((G, 8, LANES), F32),
            V((NZ, 8, LANES), F32),
            V((NY, 8, LANES), F32),
            V((NY, NZ, 16, LANES), BF16),
            V((C, 2 * LANES), BF16),
            V((NZ, 16, 2 * LANES), BF16),
            V((NZ, 16, 2 * LANES), BF16),
            V((16, 2 * LANES), F32),
            V((G, ROWS, C), BF16),
            V((NX, 16, C), BF16),
            V((G * ROWS, 2 * C), BF16),
            V((2 * ROWS, C), BF16),
            V((G, ROWS, LANES), BF16),
            V((G, ROWS, LANES), BF16),
            V((2 * C, 2 * C), BF16),
            V((2 * C, LANES), BF16),
            V((640, C), BF16),
            V((G * ROWS, LANES), BF16),
            V((2, 16, LANES), F32),
            V((16, LANES), F32),
            V((NY, 16, LANES), F32),
            V((NZ, 80, LANES), BF16),
            V((NY, LANES, LANES), BF16),
            V((NY, LANES, LANES), BF16),
            V((NZ, 16, LANES), F32),
            V((NZ, 16, LANES), F32),
            V((G, 8, LANES), F32),
            V((G, 8, LANES), F32),
            V((G, ROWS, C), F32),
            V((NX, ROWS, C), BF16),
            V((NX, ROWS, C), BF16),
            V((NX, ROWS, C), BF16),
            V((NX, ROWS, C), BF16),
            V((NX, 8, C), F32),
            V((NX, 8, C), F32),
            pltpu.SemaphoreType.DMA((CHANNELS,)),
            pltpu.SemaphoreType.DMA((CHANNELS,)),
            pltpu.SemaphoreType.DMA((5,)),
        ],
        compiler_params=pltpu.CompilerParams(
            collective_id=0, has_side_effects=True, vmem_limit_bytes=48 * 1024 * 1024
        ),
        cost_estimate=pl.CostEstimate(flops=2_000_000_000, bytes_accessed=8_000_000, transcendentals=131072),
    )(*large, clip_speaker, part_speaker, quote_bounds)
    return pl.pallas_call(
        place,
        out_shape=[jax.ShapeDtypeStruct(o.shape, o.dtype) for o in outs],
        in_specs=[pl.BlockSpec(memory_space=pl.ANY)] * 3,
        out_specs=[hbm] * 3,
        scratch_shapes=[pltpu.SemaphoreType.DMA((3,))],
        compiler_params=pltpu.CompilerParams(vmem_limit_bytes=4 * 1024 * 1024),
    )(*outs)


def solution(mesh):
    placed = (
        P("dp", "seq", None),
        P(("dp", "seq"), None),
        P("dp", None),
        P("dp", "seq", None),
        P("dp"),
        P("dp", "seq"),
        P("dp", "seq", None),
    )
    return jax.shard_map(
        body,
        mesh=mesh,
        in_specs=placed,
        out_specs=(P("dp", "seq", None), P(("dp", "seq"), None), P("dp", None)),
        check_vma=False,
    )
```

```python
import jax
import jax.numpy as jnp
from jax import lax
from jax.experimental import pallas as pl
from jax.experimental.pallas import tpu as pltpu
from jax.sharding import PartitionSpec as P

MESH = pl.DeviceIdType.MESH
F32 = jnp.float32
BF16 = jnp.bfloat16

NX, NY, NZ = 4, 8, 8
G = 8
C = 512
ROWS = 128
LANES = 128

(TILE, IDZ, WZ, WY, FILM, IDY, GOUT, ROWY, ROWZ, GWY, GWZ, GWX, HALO, PAIR, GID, GIX, EDGE) = range(17)
INP, TAB = 17, 22
CHANNELS = 27


FARTHEST = {4: (2, 1, 3), 8: (4, 3, 5, 2, 6, 1, 7)}


def iota(shape, dim):
    return lax.broadcasted_iota(jnp.int32, shape, dim)


def dot(a, b):
    return jnp.dot(a, b, preferred_element_type=F32)


def dot_nt(a, b):
    return lax.dot_general(a, b, (((1,), (1,)), ((), ())), preferred_element_type=F32)


def dot_tn(a, b):
    return lax.dot_general(a, b, (((0,), (0,)), ((), ())), preferred_element_type=F32)


def mish_slope(pre):
    t = jnp.exp(-jnp.abs(pre))
    positive = pre >= 0.0
    num = jnp.where(positive, 1.0 + 2.0 * t, t * (t + 2.0))
    rest = jnp.where(positive, 2.0 * t * t, 2.0)
    inv = 1.0 / (num + rest)
    tangent = num * inv
    gate = jnp.where(positive, 1.0, t) / (1.0 + t)
    return tangent + pre * gate * (rest * (2.0 * num + rest) * inv * inv)


def kernel(
    inp, whbm, tab, go, clip, part, qhbm, o_gi, o_gw, o_gt, w, qb,
    tsend, tg, idz, idy, wy, tabv, frs, frr, flm, xg, hx, xx, gov, gsend, gg, p01, wcat, pickt,
    gbuf, segs, c1r, yr, zr, gws, gwr, gz, gzr, gxs, gxr, pb, gis, gir, gi2, gix, esend, ed,
    ssem, rsem, lsem,
):
    z = lax.axis_index("dp")
    s = lax.axis_index("seq")
    x = lax.div(s, 16)
    y = lax.rem(lax.div(s, 2), NY)
    c = lax.rem(s, 2)
    m = 2 * x + c
    side = 2 * c - 1

    def at(zz, xx, yy, cc):
        return (zz, xx * 16 + yy * 2 + cc)

    def gpeer(i):
        return at(z, lax.div(i, 2), y, lax.rem(i, 2))

    def ypeer(i):
        return at(z, x, i, c)

    def zpeer(i):
        return at(i, x, y, c)

    def xpeer(i):
        return at(z, i, y, c)

    sibling = at(z, x, y, 1 - c)

    def hpeer(i):
        return at(z, i, lax.rem(y + side + NY, NY), 1 - c)

    def remote(src, dst, send, recv, dev):
        return pltpu.make_async_remote_copy(
            src_ref=src, dst_ref=dst, send_sem=ssem.at[send], recv_sem=rsem.at[recv],
            device_id=dev, device_id_type=MESH,
        )

    pending = []
    waiting = {}

    def watch(chan, ref):
        whole = remote(ref, ref, chan, chan, sibling)
        pending.append(whole.wait_send)
        waiting[chan] = whole.wait_recv

    def spread(chan, me, peer, src, slot, whole, n=8):
        for d in FARTHEST[n]:
            i = lax.rem(me + d, n)
            remote(src(i), slot(me), chan, chan, peer(i)).start()

        watch(chan, whole)

    def collect(chan):
        waiting.pop(chan)()

    def x_spread(base, src, slot, slots):
        for d in FARTHEST[NX]:
            remote(src, slot(x, c), base, base + d, xpeer(lax.rem(x + d, NX))).start()

        remote(src, slot(x, c), base, base, sibling).start()
        pending.append(remote(slots(4), slots(4), base, base, sibling).wait_send)
        waiting[base] = remote(slot(x, 1 - c), slot(x, 1 - c), base, base, sibling).wait_recv
        for d in range(1, NX):
            mine = slot(lax.rem(x + NX - d, NX), c)
            waiting[base + d] = remote(mine, mine, base, base + d, sibling).wait_recv

    def x_hand_on(base, slot, slots):
        for d in (1, 3, 2):
            collect(base + d)
            mine = slot(lax.rem(x + NX - d, NX), c)
            remote(mine, mine, base + 4, base + 4, sibling).start()

        watch(base + 4, slots(3))

    def column(i, cc):
        return o_gt.at[:, pl.ds(pl.multiple_of(cc * C + i * LANES, LANES), LANES)]

    def columns(n):
        return o_gt.at[:, pl.ds(0, n * LANES)]

    barrier = pltpu.get_barrier_semaphore()

    for d in FARTHEST[8]:
        pl.semaphore_signal(barrier, inc=1, device_id=zpeer(lax.rem(z + d, NZ)), device_id_type=MESH)
        pl.semaphore_signal(barrier, inc=1, device_id=ypeer(lax.rem(y + d, NY)), device_id_type=MESH)
    for i in range(NX):
        pl.semaphore_signal(barrier, inc=1, device_id=hpeer(i), device_id_type=MESH)
    for d in FARTHEST[8]:
        pl.semaphore_signal(barrier, inc=1, device_id=gpeer(lax.rem(m + d, G)), device_id_type=MESH)

    xcol = pl.multiple_of(x * LANES, LANES)
    scol = pl.multiple_of(C + x * LANES, LANES)
    get_go = pltpu.make_async_copy(go.at[0], gov, lsem.at[0])
    get_in = pltpu.make_async_copy(inp.at[0], xg.at[m], lsem.at[1])
    get_scale = pltpu.make_async_copy(tab.at[:, pl.ds(xcol, LANES)], tabv.at[:, pl.ds(0, LANES)], lsem.at[2])
    get_shift = pltpu.make_async_copy(tab.at[:, pl.ds(scol, LANES)], tabv.at[:, pl.ds(LANES, LANES)], lsem.at[3])
    get_w = pltpu.make_async_copy(whbm, w, lsem.at[4])
    get_qb = pltpu.make_async_copy(qhbm, qb, lsem.at[5])
    for copy in (get_w, get_qb, get_go, get_in, get_scale, get_shift):
        copy.start()

    row8 = iota((8, LANES), 0)
    lane = iota((8, LANES), 1)
    info = jnp.where(lane == 0, part[0, 0], 0)
    get_qb.wait()
    info = jnp.where(lane == 1, qb[0, 0, 0], info)
    info = jnp.where(lane == 2, qb[0, 0, 1], info)
    info = jnp.where(lane == 3, clip[0], info).astype(F32)
    get_w.wait()
    wrow = w[...].astype(F32)
    for i in range(G):
        qi, ci = i // 2, i % 2
        taps = (1, 3) if ci == 0 else (2, 0)
        first, second = [wrow[:, k * C + qi * LANES : k * C + (qi + 1) * LANES] for k in taps]
        tsend[i] = jnp.where(row8 == 0, first, jnp.where(row8 == 1, second, info))
    tg[m] = tsend[m]

    pl.semaphore_wait(barrier, 25)

    spread(TILE, m, gpeer, lambda i: tsend.at[i], lambda i: tg.at[i], tg.at[pl.ds(0, 7)])

    def frame_slot(i, cc):
        return xg.at[2 * i + cc]

    def frame_slots(n):
        return xg.at[pl.ds(0, n)]

    turn = (c * ((y + 1) // NY) + (1 - c) * (3 * ((NY - y) // NY))) % NX

    get_go.wait()
    ri, rj = iota((256, 256), 0), iota((256, 256), 1)
    pick = jnp.where(ri < ROWS, 2 * ri, 2 * (ri - ROWS) + 1)
    gde = dot(jnp.where(rj == pick, 1.0, 0.0).astype(BF16), gov[...]).astype(BF16)
    for i in range(G):
        qi, ci = i // 2, i % 2
        gsend[i] = gde[ci * ROWS : (ci + 1) * ROWS, qi * LANES : (qi + 1) * LANES]
    gg[m] = gsend[m]

    collect(TILE)
    rows_a = jnp.zeros((8, LANES), F32)
    rows_b = rows_a
    ids = rows_a
    for i in range(G):
        tile = tg[i]
        rows_a = jnp.where(row8 == i, tile[0:1], rows_a)
        rows_b = jnp.where(row8 == i, tile[1:2], rows_b)
        ids = jnp.where(row8 == i, tile[2:3], ids)
    idz[z] = ids
    wy[y, z] = jnp.concatenate([rows_a, rows_b], 0).astype(BF16)
    spread(WZ, z, zpeer, lambda i: wy.at[y, z], lambda i: wy.at[y, i], wy.at[y, pl.ds(0, 7)])
    spread(IDZ, z, zpeer, lambda i: idz.at[z], lambda i: idz.at[i], idz.at[pl.ds(0, 7)])
    x_spread(INP, inp.at[0], frame_slot, frame_slots)
    @pl.loop(0, NX)
    def _(i):
        src = inp.at[0, pl.ds(pl.multiple_of(c * 112, 16), 16), :]
        remote(src, hx.at[(x + turn) % NX], HALO, HALO, hpeer(i)).start()

    watch(HALO, hx)

    spread(GOUT, m, gpeer, lambda i: gsend.at[i], lambda i: gg.at[i], gg.at[pl.ds(0, 7)])

    @pl.loop(0, 8)
    def _(b):
        row = b * LANES + iota((LANES, LANES), 0)
        place = ((row >> 1) & 7) * 128 + ((row >> 6) & 7) * 16 + (row >> 9) * 8 + ((row >> 4) & 3) * 2 + (row & 1)
        off = place - iota((LANES, LANES), 1)
        for k in range(8):
            p01[pl.ds(pl.multiple_of(b * LANES, LANES), LANES), k * LANES : (k + 1) * LANES] = jnp.where(
                off == k * LANES, 1.0, 0.0
            ).astype(BF16)

    collect(WZ)
    spread(WY, y, ypeer, lambda i: wy.at[y], lambda i: wy.at[i], wy.at[pl.ds(0, 7)])

    collect(IDZ)
    base = (z * C).astype(F32)
    lane512 = iota((8, C), 1).astype(F32)
    packed = jnp.zeros((8, LANES), F32)
    asked = []
    for i in range(NZ):
        tile = idz[i]
        part_id, clip_id = tile[:, 0:1], tile[:, 3:4]
        asked.append(jnp.where(part_id - base == lane512, 1.0, 0.0))
        asked.append(jnp.where(clip_id - base == lane512, 1.0, 0.0))
        packed = jnp.where(lane == i, part_id, jnp.where(lane == 8 + i, clip_id, packed))
    idy[y] = packed
    spread(IDY, y, ypeer, lambda i: idy.at[y], lambda i: idy.at[i], idy.at[pl.ds(0, 7)])
    get_scale.wait()
    get_shift.wait()
    served = dot(jnp.concatenate(asked, 0).astype(BF16), tabv[...]).astype(BF16)
    for i in range(NZ):
        frs[i] = served[16 * i : 16 * (i + 1)]
    frr[z] = frs[z]
    spread(FILM, z, zpeer, lambda i: frs.at[i], lambda i: frr.at[i], frr.at[pl.ds(0, 7)])

    x_hand_on(INP, frame_slot, frame_slots)
    get_in.wait()
    collect(INP)
    collect(INP + 4)
    collect(HALO)

    shift = jnp.where(rj - ri == side, 1.0, 0.0).astype(BF16)
    rowp = iota((256, C), 0)
    for i in range(NX):
        pair = xg[2 * i : 2 * i + 2].reshape(256, C)
        block = hx[i].astype(F32)
        outer = jnp.where(c == 0, block[15:16], block[0:1])
        inside = i * 16 + y * 2 + c != c * 63
        outer = jnp.where(inside, outer, 0.0)
        moved = jnp.where(rowp == c * 255, outer, dot(shift, pair))
        xx[256 * i : 256 * (i + 1)] = (dot(pair, p01[0:C]) + dot(moved.astype(BF16), p01[C : 2 * C])).astype(BF16)

    collect(FILM)
    film = frr[0].astype(F32)
    for i in range(1, NZ):
        film = film + frr[i].astype(F32)
    flm[...] = film
    collect(GOUT)
    collect(WY)

    arrived = wy[...].reshape(2 * C, LANES)
    base_row = flm[8:9]
    frame = (2 * iota((ROWS, LANES), 0) + c).astype(F32)
    part_scale = jnp.zeros((8, LANES), F32)
    part_shift = part_scale
    base_scale = jnp.zeros((1, LANES), F32)
    base_shift = base_scale
    for i in range(G):
        if i % 2 == 0:
            u_pair = dot(xx[ROWS * i : ROWS * (i + 2)], arrived)
        u = u_pair[ROWS * (i % 2) : ROWS * (i % 2 + 1)]
        bounds = tg[i]
        quoted = (frame >= bounds[2:3, 1:2]) & (frame < bounds[2:3, 2:3])
        scale = jnp.where(quoted, flm[i : i + 1, 0:LANES], base_row[:, 0:LANES])
        offset = jnp.where(quoted, flm[i : i + 1, LANES:], base_row[:, LANES:])
        gain = 1.0 + scale
        grad = gg[i].astype(F32) * mish_slope(u * gain + offset)
        gbuf[ROWS * i : ROWS * (i + 1)] = (grad * gain).astype(BF16)
        gu = grad * u
        part_scale = jnp.where(row8 == i, jnp.sum(jnp.where(quoted, gu, 0.0), 0, keepdims=True), part_scale)
        part_shift = jnp.where(row8 == i, jnp.sum(jnp.where(quoted, grad, 0.0), 0, keepdims=True), part_shift)
        base_scale = base_scale + jnp.sum(jnp.where(quoted, 0.0, gu), 0, keepdims=True)
        base_shift = base_shift + jnp.sum(jnp.where(quoted, 0.0, grad), 0, keepdims=True)
    fscale = 1.0 / 16.0
    segs[0] = jnp.concatenate([part_scale, jnp.where(row8 == 0, base_scale, 0.0)], 0) * fscale
    segs[1] = jnp.concatenate([part_shift, jnp.where(row8 == 0, base_shift, 0.0)], 0) * fscale
    remote(segs.at[1 - c], c1r, PAIR, PAIR, sibling).start()
    watch(PAIR, c1r)

    gwp = dot_tn(gbuf[...], xx[...]).astype(BF16)
    for i in range(NY):
        gws[i] = gwp[:, LANES * i : LANES * (i + 1)]

    collect(PAIR)
    yr[y] = segs[c] + c1r[...]
    spread(ROWY, y, ypeer, lambda i: yr.at[y], lambda i: yr.at[i], yr.at[pl.ds(0, 7)])
    gwr[y] = gws[y]
    spread(GWY, y, ypeer, lambda i: gws.at[i], lambda i: gwr.at[i], gwr.at[pl.ds(0, 7)])

    wcat[...] = dot(p01[...], arrived).astype(BF16)
    back = jnp.where(ri - rj == side, 1.0, 0.0).astype(BF16)
    edges = jnp.zeros((8, LANES), F32)
    for i in range(NX):
        pair = gbuf[256 * i : 256 * (i + 1)]
        moved = dot(back, pair).astype(BF16)
        grads = dot_nt(pair, wcat[0:C]) + dot_nt(moved, wcat[C : 2 * C])
        pb[2 * i] = grads[0:ROWS]
        pb[2 * i + 1] = grads[ROWS:]
        gis[i] = pb[2 * i + 1 - c].astype(BF16)
        remote(gis.at[i], gir.at[i], GID, GID, sibling).start()
        outer = jnp.where(c == 0, pair[0:16].astype(F32)[0:1], pair[240:256].astype(F32)[15:16])
        edges = jnp.where(row8 == i, outer, edges)
    watch(GID, gir)
    edge_rows = dot_nt(edges.astype(BF16), wcat[C : 2 * C])

    for i in range(NX):
        esend[i] = jnp.broadcast_to(edge_rows[i : i + 1], (8, C))

    @pl.loop(0, NX)
    def _(i):
        remote(esend.at[i], ed.at[x], EDGE, EDGE, hpeer((i + turn) % NX)).start()

    watch(EDGE, ed)
    collect(IDY)
    for i in range(NZ):
        for k in range(NY):
            match = jnp.where(idy[k][:, i : i + 1] - base == lane512, 1.0, 0.0)
            if k % 2 == 0:
                even = match
            else:
                pickt[80 * i + 8 * (k - 1) : 80 * i + 8 * (k + 1)] = jnp.concatenate([even, match], 0).astype(BF16)
        match = jnp.where(idy[0][:, 8 + i : 9 + i] - base == lane512, 1.0, 0.0)
        pickt[80 * i + 64 : 80 * i + 80] = jnp.concatenate([match, match], 0).astype(BF16)

    collect(ROWY)
    sums = yr[0, 8:16]
    for i in range(1, NY):
        sums = sums + yr[i, 8:16]
    pieces = [yr[i, 0:8] for i in range(NY)] + [sums, jnp.zeros((8, LANES), F32)]
    zr[z] = jnp.concatenate(pieces, 0).astype(BF16)
    spread(ROWZ, z, zpeer, lambda i: zr.at[z], lambda i: zr.at[i], zr.at[pl.ds(0, 7)])

    collect(GID)
    for i in range(NX):
        total = pb[2 * i + c] + gir[i].astype(F32)
        pb[2 * i + c] = total
        gi2[i] = total.astype(BF16)
    spread(GIX, x, xpeer, lambda i: gi2.at[i], lambda i: gix.at[i], gix.at[pl.ds(0, 3)], n=NX)

    collect(GWY)
    gsum = gwr[0].astype(F32)
    for i in range(1, NY):
        gsum = gsum + gwr[i].astype(F32)
    turned = gsum.T
    for i in range(NZ):
        gz[i] = turned[16 * i : 16 * (i + 1)]
    gzr[z] = gz[z]
    spread(GWZ, z, zpeer, lambda i: gz.at[i], lambda i: gzr.at[i], gzr.at[pl.ds(0, 7)])

    ocol = pl.multiple_of(c * C + x * LANES, LANES)
    collect(ROWZ)
    o_gt[:, pl.ds(ocol, LANES)] = dot_tn(pickt[...], zr[...].reshape(640, LANES)).astype(BF16)
    x_spread(TAB, column(x, c), column, columns)

    collect(GWZ)
    gsum = gzr[0]
    for i in range(1, NZ):
        gsum = gsum + gzr[i]
    gsum = gsum * (1.0 / 256.0)
    for i in range(G):
        gxs[i] = jnp.where(row8 == 0, gsum[i : i + 1], gsum[8 + i : 9 + i])
    gxr[m] = gxs[m]
    spread(GWX, m, gpeer, lambda i: gxs.at[i], lambda i: gxr.at[i], gxr.at[pl.ds(0, 7)])

    collect(GIX)
    collect(EDGE)
    gix[x] = jnp.zeros((ROWS, C), BF16)
    total = pb[2 * x + c]
    edge = ed[0, 0:1]
    for i in range(NX):
        total = total + gix[i].astype(F32)
        if i:
            edge = edge + ed[i, 0:1]
    edge = jnp.where(s != c * 63, edge, 0.0)
    total = total + jnp.where(iota((ROWS, C), 0) == c * 127, edge, 0.0)
    o_gi[0] = total.astype(BF16)

    x_hand_on(TAB, column, columns)
    collect(GWX)
    for i in range(G):
        qi, ci = i // 2, i % 2
        taps = (1, 3) if ci == 0 else (2, 0)
        for t, k in enumerate(taps):
            o_gw[:, k * C + qi * LANES : k * C + (qi + 1) * LANES] = gxr[i, t : t + 1]
    collect(TAB)
    collect(TAB + 4)

    for finish in pending:
        finish()


def place(gi, gw, gt, o_gi, o_gw, o_gt, sem):
    copies = [pltpu.make_async_copy(a, b, sem.at[k]) for k, (a, b) in enumerate(((gt, o_gt), (gi, o_gi), (gw, o_gw)))]
    for copy in copies:
        copy.start()
    for copy in copies:
        copy.wait()


def body(inputs, weight, table, grad_out, clip_speaker, part_speaker, quote_bounds):
    vmem = pl.BlockSpec(memory_space=pltpu.VMEM)
    hbm = pl.BlockSpec(memory_space=pltpu.HBM)
    smem = pl.BlockSpec(memory_space=pltpu.SMEM)
    V = pltpu.VMEM
    large = [pltpu.with_memory_space_constraint(a, pltpu.HBM) for a in (inputs, weight, table, grad_out, quote_bounds)]
    outs = pl.pallas_call(
        kernel,
        out_shape=(
            jax.ShapeDtypeStruct(inputs.shape, BF16),
            jax.ShapeDtypeStruct(weight.shape, F32),
            jax.ShapeDtypeStruct(table.shape, BF16),
        ),
        in_specs=[hbm] * 4 + [smem] * 2 + [hbm],
        out_specs=(vmem, vmem, vmem),
        scratch_shapes=[
            V((1, 4 * C), BF16),
            pltpu.SMEM((1, 1, 2), jnp.int32),
            V((G, 8, LANES), F32),
            V((G, 8, LANES), F32),
            V((NZ, 8, LANES), F32),
            V((NY, 8, LANES), F32),
            V((NY, NZ, 16, LANES), BF16),
            V((C, 2 * LANES), BF16),
            V((NZ, 16, 2 * LANES), BF16),
            V((NZ, 16, 2 * LANES), BF16),
            V((16, 2 * LANES), F32),
            V((G, ROWS, C), BF16),
            V((NX, 16, C), BF16),
            V((G * ROWS, 2 * C), BF16),
            V((2 * ROWS, C), BF16),
            V((G, ROWS, LANES), BF16),
            V((G, ROWS, LANES), BF16),
            V((2 * C, 2 * C), BF16),
            V((2 * C, LANES), BF16),
            V((640, C), BF16),
            V((G * ROWS, LANES), BF16),
            V((2, 16, LANES), F32),
            V((16, LANES), F32),
            V((NY, 16, LANES), F32),
            V((NZ, 80, LANES), BF16),
            V((NY, LANES, LANES), BF16),
            V((NY, LANES, LANES), BF16),
            V((NZ, 16, LANES), F32),
            V((NZ, 16, LANES), F32),
            V((G, 8, LANES), F32),
            V((G, 8, LANES), F32),
            V((G, ROWS, C), F32),
            V((NX, ROWS, C), BF16),
            V((NX, ROWS, C), BF16),
            V((NX, ROWS, C), BF16),
            V((NX, ROWS, C), BF16),
            V((NX, 8, C), F32),
            V((NX, 8, C), F32),
            pltpu.SemaphoreType.DMA((CHANNELS,)),
            pltpu.SemaphoreType.DMA((CHANNELS,)),
            pltpu.SemaphoreType.DMA((6,)),
        ],
        compiler_params=pltpu.CompilerParams(
            collective_id=0, has_side_effects=True, vmem_limit_bytes=48 * 1024 * 1024
        ),
        cost_estimate=pl.CostEstimate(flops=2_000_000_000, bytes_accessed=8_000_000, transcendentals=131072),
    )(*large[:4], clip_speaker, part_speaker, large[4])
    return pl.pallas_call(
        place,
        out_shape=[jax.ShapeDtypeStruct(o.shape, o.dtype) for o in outs],
        in_specs=[pl.BlockSpec(memory_space=pl.ANY)] * 3,
        out_specs=[hbm] * 3,
        scratch_shapes=[pltpu.SemaphoreType.DMA((3,))],
        compiler_params=pltpu.CompilerParams(vmem_limit_bytes=4 * 1024 * 1024),
    )(*outs)


def solution(mesh):
    placed = (
        P("dp", "seq", None),
        P(("dp", "seq"), None),
        P("dp", None),
        P("dp", "seq", None),
        P("dp"),
        P("dp", "seq"),
        P("dp", "seq", None),
    )
    return jax.shard_map(
        body,
        mesh=mesh,
        in_specs=placed,
        out_specs=(P("dp", "seq", None), P(("dp", "seq"), None), P("dp", None)),
        check_vma=False,
    )
```

```python
import jax
import jax.numpy as jnp
from jax import lax
from jax.experimental import pallas as pl
from jax.experimental.pallas import tpu as pltpu
from jax.sharding import PartitionSpec as P

MESH = pl.DeviceIdType.MESH
F32 = jnp.float32
BF16 = jnp.bfloat16

NX, NY, NZ = 4, 8, 8
G = 8
C = 512
ROWS = 128
LANES = 128

(TILE, IDZ, WZ, WY, FILM, IDY, GOUT, ROWY, ROWZ, GWY, GWZ, GWX, HALO, PAIR, GID, GIX, EDGE) = range(17)
INP, TAB = 17, 22
CHANNELS = 27


FARTHEST = {4: (2, 1, 3), 8: (4, 3, 5, 2, 6, 1, 7)}


def iota(shape, dim):
    return lax.broadcasted_iota(jnp.int32, shape, dim)


def dot(a, b):
    return jnp.dot(a, b, preferred_element_type=F32)


def dot_nt(a, b):
    return lax.dot_general(a, b, (((1,), (1,)), ((), ())), preferred_element_type=F32)


def dot_tn(a, b):
    return lax.dot_general(a, b, (((0,), (0,)), ((), ())), preferred_element_type=F32)


def mish_slope(pre):
    t = jnp.exp(-jnp.abs(pre))
    positive = pre >= 0.0
    num = jnp.where(positive, 1.0 + 2.0 * t, t * (t + 2.0))
    rest = jnp.where(positive, 2.0 * t * t, 2.0)
    inv = 1.0 / (num + rest)
    tangent = num * inv
    gate = jnp.where(positive, 1.0, t) / (1.0 + t)
    return tangent + pre * gate * (rest * (2.0 * num + rest) * inv * inv)


def kernel(
    inp, whbm, tab, go, clip, part, qhbm, o_gi, o_gw, o_gt, w, qb,
    tsend, tg, idz, idy, wy, tabv, frs, frr, flm, xg, hx, xx, gov, gsend, gg, p01, wcat, pickt,
    gbuf, segs, c1r, yr, zr, gws, gwr, gz, gzr, gxs, gxr, pb, gis, gir, gi2, gix, esend, ed,
    ssem, rsem, lsem,
):
    z = lax.axis_index("dp")
    s = lax.axis_index("seq")
    x = lax.div(s, 16)
    y = lax.rem(lax.div(s, 2), NY)
    c = lax.rem(s, 2)
    m = 2 * x + c
    side = 2 * c - 1

    def at(zz, xx, yy, cc):
        return (zz, xx * 16 + yy * 2 + cc)

    def gpeer(i):
        return at(z, lax.div(i, 2), y, lax.rem(i, 2))

    def ypeer(i):
        return at(z, x, i, c)

    def zpeer(i):
        return at(i, x, y, c)

    def xpeer(i):
        return at(z, i, y, c)

    sibling = at(z, x, y, 1 - c)

    def hpeer(i):
        return at(z, i, lax.rem(y + side + NY, NY), 1 - c)

    def remote(src, dst, send, recv, dev):
        return pltpu.make_async_remote_copy(
            src_ref=src, dst_ref=dst, send_sem=ssem.at[send], recv_sem=rsem.at[recv],
            device_id=dev, device_id_type=MESH,
        )

    pending = []
    waiting = {}

    def watch(chan, ref):
        whole = remote(ref, ref, chan, chan, sibling)
        pending.append(whole.wait_send)
        waiting[chan] = whole.wait_recv

    def spread(chan, me, peer, src, slot, whole, n=8):
        for d in FARTHEST[n]:
            i = lax.rem(me + d, n)
            remote(src(i), slot(me), chan, chan, peer(i)).start()

        watch(chan, whole)

    def collect(chan):
        waiting.pop(chan)()

    def x_spread(base, src, slot, slots):
        for d in FARTHEST[NX]:
            remote(src, slot(x, c), base, base + d, xpeer(lax.rem(x + d, NX))).start()

        remote(src, slot(x, c), base, base, sibling).start()
        pending.append(remote(slots(4), slots(4), base, base, sibling).wait_send)
        waiting[base] = remote(slot(x, 1 - c), slot(x, 1 - c), base, base, sibling).wait_recv
        for d in range(1, NX):
            mine = slot(lax.rem(x + NX - d, NX), c)
            waiting[base + d] = remote(mine, mine, base, base + d, sibling).wait_recv

    def x_hand_on(base, slot, slots):
        for d in (1, 3, 2):
            collect(base + d)
            mine = slot(lax.rem(x + NX - d, NX), c)
            remote(mine, mine, base + 4, base + 4, sibling).start()

        watch(base + 4, slots(3))

    def column(i, cc):
        return o_gt.at[:, pl.ds(pl.multiple_of(cc * C + i * LANES, LANES), LANES)]

    def columns(n):
        return o_gt.at[:, pl.ds(0, n * LANES)]

    barrier = pltpu.get_barrier_semaphore()

    for d in FARTHEST[8]:
        pl.semaphore_signal(barrier, inc=1, device_id=zpeer(lax.rem(z + d, NZ)), device_id_type=MESH)
        pl.semaphore_signal(barrier, inc=1, device_id=ypeer(lax.rem(y + d, NY)), device_id_type=MESH)
    for i in range(NX):
        pl.semaphore_signal(barrier, inc=1, device_id=hpeer(i), device_id_type=MESH)
    for d in FARTHEST[8]:
        pl.semaphore_signal(barrier, inc=1, device_id=gpeer(lax.rem(m + d, G)), device_id_type=MESH)

    xcol = pl.multiple_of(x * LANES, LANES)
    scol = pl.multiple_of(C + x * LANES, LANES)
    get_go = pltpu.make_async_copy(go.at[0], gov, lsem.at[0])
    get_in = pltpu.make_async_copy(inp.at[0], xg.at[m], lsem.at[1])
    get_scale = pltpu.make_async_copy(tab.at[:, pl.ds(xcol, LANES)], tabv.at[:, pl.ds(0, LANES)], lsem.at[2])
    get_shift = pltpu.make_async_copy(tab.at[:, pl.ds(scol, LANES)], tabv.at[:, pl.ds(LANES, LANES)], lsem.at[3])
    get_w = pltpu.make_async_copy(whbm, w, lsem.at[4])
    get_qb = pltpu.make_async_copy(qhbm, qb, lsem.at[5])
    for copy in (get_w, get_qb, get_go, get_in, get_scale, get_shift):
        copy.start()

    row8 = iota((8, LANES), 0)
    lane = iota((8, LANES), 1)
    info = jnp.where(lane == 0, part[0, 0], 0)
    get_qb.wait()
    info = jnp.where(lane == 1, qb[0, 0, 0], info)
    info = jnp.where(lane == 2, qb[0, 0, 1], info)
    info = jnp.where(lane == 3, clip[0], info).astype(F32)
    get_w.wait()
    wrow = w[...].astype(F32)
    for i in range(G):
        qi, ci = i // 2, i % 2
        taps = (1, 3) if ci == 0 else (2, 0)
        first, second = [wrow[:, k * C + qi * LANES : k * C + (qi + 1) * LANES] for k in taps]
        tsend[i] = jnp.where(row8 == 0, first, jnp.where(row8 == 1, second, info))
    tg[m] = tsend[m]

    pl.semaphore_wait(barrier, 25)

    spread(TILE, m, gpeer, lambda i: tsend.at[i], lambda i: tg.at[i], tg.at[pl.ds(0, 7)])

    def frame_slot(i, cc):
        return xg.at[2 * i + cc]

    def frame_slots(n):
        return xg.at[pl.ds(0, n)]

    turn = (c * ((y + 1) // NY) + (1 - c) * (3 * ((NY - y) // NY))) % NX

    get_go.wait()
    ri, rj = iota((256, 256), 0), iota((256, 256), 1)
    pick = jnp.where(ri < ROWS, 2 * ri, 2 * (ri - ROWS) + 1)
    gde = dot(jnp.where(rj == pick, 1.0, 0.0).astype(BF16), gov[...]).astype(BF16)
    for i in range(G):
        qi, ci = i // 2, i % 2
        gsend[i] = gde[ci * ROWS : (ci + 1) * ROWS, qi * LANES : (qi + 1) * LANES]
    gg[m] = gsend[m]

    collect(TILE)
    rows_a = jnp.zeros((8, LANES), F32)
    rows_b = rows_a
    ids = rows_a
    for i in range(G):
        tile = tg[i]
        rows_a = jnp.where(row8 == i, tile[0:1], rows_a)
        rows_b = jnp.where(row8 == i, tile[1:2], rows_b)
        ids = jnp.where(row8 == i, tile[2:3], ids)
    idz[z] = ids
    wy[y, z] = jnp.concatenate([rows_a, rows_b], 0).astype(BF16)
    spread(IDZ, z, zpeer, lambda i: idz.at[z], lambda i: idz.at[i], idz.at[pl.ds(0, 7)])
    spread(WZ, z, zpeer, lambda i: wy.at[y, z], lambda i: wy.at[y, i], wy.at[y, pl.ds(0, 7)])
    x_spread(INP, inp.at[0], frame_slot, frame_slots)
    @pl.loop(0, NX)
    def _(i):
        src = inp.at[0, pl.ds(pl.multiple_of(c * 112, 16), 16), :]
        remote(src, hx.at[(x + turn) % NX], HALO, HALO, hpeer(i)).start()

    watch(HALO, hx)

    spread(GOUT, m, gpeer, lambda i: gsend.at[i], lambda i: gg.at[i], gg.at[pl.ds(0, 7)])

    @pl.loop(0, 8)
    def _(b):
        row = b * LANES + iota((LANES, LANES), 0)
        place = ((row >> 1) & 7) * 128 + ((row >> 6) & 7) * 16 + (row >> 9) * 8 + ((row >> 4) & 3) * 2 + (row & 1)
        off = place - iota((LANES, LANES), 1)
        for k in range(8):
            p01[pl.ds(pl.multiple_of(b * LANES, LANES), LANES), k * LANES : (k + 1) * LANES] = jnp.where(
                off == k * LANES, 1.0, 0.0
            ).astype(BF16)

    collect(WZ)
    spread(WY, y, ypeer, lambda i: wy.at[y], lambda i: wy.at[i], wy.at[pl.ds(0, 7)])

    collect(IDZ)
    base = (z * C).astype(F32)
    lane512 = iota((8, C), 1).astype(F32)
    packed = jnp.zeros((8, LANES), F32)
    asked = []
    for i in range(NZ):
        tile = idz[i]
        part_id, clip_id = tile[:, 0:1], tile[:, 3:4]
        asked.append(jnp.where(part_id - base == lane512, 1.0, 0.0))
        asked.append(jnp.where(clip_id - base == lane512, 1.0, 0.0))
        packed = jnp.where(lane == i, part_id, jnp.where(lane == 8 + i, clip_id, packed))
    idy[y] = packed
    get_scale.wait()
    get_shift.wait()
    served = dot(jnp.concatenate(asked, 0).astype(BF16), tabv[...]).astype(BF16)
    for i in range(NZ):
        frs[i] = served[16 * i : 16 * (i + 1)]
    frr[z] = frs[z]
    spread(FILM, z, zpeer, lambda i: frs.at[i], lambda i: frr.at[i], frr.at[pl.ds(0, 7)])
    spread(IDY, y, ypeer, lambda i: idy.at[y], lambda i: idy.at[i], idy.at[pl.ds(0, 7)])

    x_hand_on(INP, frame_slot, frame_slots)
    get_in.wait()
    collect(INP)
    collect(INP + 4)
    collect(HALO)

    shift = jnp.where(rj - ri == side, 1.0, 0.0).astype(BF16)
    rowp = iota((256, C), 0)
    for i in range(NX):
        pair = xg[2 * i : 2 * i + 2].reshape(256, C)
        block = hx[i].astype(F32)
        outer = jnp.where(c == 0, block[15:16], block[0:1])
        inside = i * 16 + y * 2 + c != c * 63
        outer = jnp.where(inside, outer, 0.0)
        moved = jnp.where(rowp == c * 255, outer, dot(shift, pair))
        xx[256 * i : 256 * (i + 1)] = (dot(pair, p01[0:C]) + dot(moved.astype(BF16), p01[C : 2 * C])).astype(BF16)

    collect(FILM)
    film = frr[0].astype(F32)
    for i in range(1, NZ):
        film = film + frr[i].astype(F32)
    flm[...] = film
    collect(GOUT)
    collect(WY)

    arrived = wy[...].reshape(2 * C, LANES)
    base_row = flm[8:9]
    frame = (2 * iota((ROWS, LANES), 0) + c).astype(F32)
    part_scale = jnp.zeros((8, LANES), F32)
    part_shift = part_scale
    base_scale = jnp.zeros((1, LANES), F32)
    base_shift = base_scale
    for i in range(G):
        if i % 2 == 0:
            u_pair = dot(xx[ROWS * i : ROWS * (i + 2)], arrived)
        u = u_pair[ROWS * (i % 2) : ROWS * (i % 2 + 1)]
        bounds = tg[i]
        quoted = (frame >= bounds[2:3, 1:2]) & (frame < bounds[2:3, 2:3])
        scale = jnp.where(quoted, flm[i : i + 1, 0:LANES], base_row[:, 0:LANES])
        offset = jnp.where(quoted, flm[i : i + 1, LANES:], base_row[:, LANES:])
        gain = 1.0 + scale
        grad = gg[i].astype(F32) * mish_slope(u * gain + offset)
        gbuf[ROWS * i : ROWS * (i + 1)] = (grad * gain).astype(BF16)
        gu = grad * u
        part_scale = jnp.where(row8 == i, jnp.sum(jnp.where(quoted, gu, 0.0), 0, keepdims=True), part_scale)
        part_shift = jnp.where(row8 == i, jnp.sum(jnp.where(quoted, grad, 0.0), 0, keepdims=True), part_shift)
        base_scale = base_scale + jnp.sum(jnp.where(quoted, 0.0, gu), 0, keepdims=True)
        base_shift = base_shift + jnp.sum(jnp.where(quoted, 0.0, grad), 0, keepdims=True)
    fscale = 1.0 / 16.0
    segs[0] = jnp.concatenate([part_scale, jnp.where(row8 == 0, base_scale, 0.0)], 0) * fscale
    segs[1] = jnp.concatenate([part_shift, jnp.where(row8 == 0, base_shift, 0.0)], 0) * fscale
    remote(segs.at[1 - c], c1r, PAIR, PAIR, sibling).start()
    watch(PAIR, c1r)

    gwp = dot_tn(gbuf[...], xx[...]).astype(BF16)
    for i in range(NY):
        gws[i] = gwp[:, LANES * i : LANES * (i + 1)]

    collect(PAIR)
    yr[y] = segs[c] + c1r[...]
    spread(ROWY, y, ypeer, lambda i: yr.at[y], lambda i: yr.at[i], yr.at[pl.ds(0, 7)])
    gwr[y] = gws[y]
    spread(GWY, y, ypeer, lambda i: gws.at[i], lambda i: gwr.at[i], gwr.at[pl.ds(0, 7)])

    wcat[...] = dot(p01[...], arrived).astype(BF16)
    back = jnp.where(ri - rj == side, 1.0, 0.0).astype(BF16)
    edges = jnp.zeros((8, LANES), F32)
    for i in range(NX):
        pair = gbuf[256 * i : 256 * (i + 1)]
        moved = dot(back, pair).astype(BF16)
        grads = dot_nt(pair, wcat[0:C]) + dot_nt(moved, wcat[C : 2 * C])
        pb[2 * i] = grads[0:ROWS]
        pb[2 * i + 1] = grads[ROWS:]
        gis[i] = pb[2 * i + 1 - c].astype(BF16)
        remote(gis.at[i], gir.at[i], GID, GID, sibling).start()
        outer = jnp.where(c == 0, pair[0:16].astype(F32)[0:1], pair[240:256].astype(F32)[15:16])
        edges = jnp.where(row8 == i, outer, edges)
    watch(GID, gir)
    edge_rows = dot_nt(edges.astype(BF16), wcat[C : 2 * C])

    for i in range(NX):
        esend[i] = jnp.broadcast_to(edge_rows[i : i + 1], (8, C))

    @pl.loop(0, NX)
    def _(i):
        remote(esend.at[i], ed.at[x], EDGE, EDGE, hpeer((i + turn) % NX)).start()

    watch(EDGE, ed)
    collect(IDY)
    for i in range(NZ):
        for k in range(NY):
            match = jnp.where(idy[k][:, i : i + 1] - base == lane512, 1.0, 0.0)
            if k % 2 == 0:
                even = match
            else:
                pickt[80 * i + 8 * (k - 1) : 80 * i + 8 * (k + 1)] = jnp.concatenate([even, match], 0).astype(BF16)
        match = jnp.where(idy[0][:, 8 + i : 9 + i] - base == lane512, 1.0, 0.0)
        pickt[80 * i + 64 : 80 * i + 80] = jnp.concatenate([match, match], 0).astype(BF16)

    collect(ROWY)
    sums = yr[0, 8:16]
    for i in range(1, NY):
        sums = sums + yr[i, 8:16]
    pieces = [yr[i, 0:8] for i in range(NY)] + [sums, jnp.zeros((8, LANES), F32)]
    zr[z] = jnp.concatenate(pieces, 0).astype(BF16)
    spread(ROWZ, z, zpeer, lambda i: zr.at[z], lambda i: zr.at[i], zr.at[pl.ds(0, 7)])

    collect(GID)
    for i in range(NX):
        total = pb[2 * i + c] + gir[i].astype(F32)
        pb[2 * i + c] = total
        gi2[i] = total.astype(BF16)
    spread(GIX, x, xpeer, lambda i: gi2.at[i], lambda i: gix.at[i], gix.at[pl.ds(0, 3)], n=NX)

    collect(GWY)
    gsum = gwr[0].astype(F32)
    for i in range(1, NY):
        gsum = gsum + gwr[i].astype(F32)
    turned = gsum.T
    for i in range(NZ):
        gz[i] = turned[16 * i : 16 * (i + 1)]
    gzr[z] = gz[z]
    spread(GWZ, z, zpeer, lambda i: gz.at[i], lambda i: gzr.at[i], gzr.at[pl.ds(0, 7)])

    ocol = pl.multiple_of(c * C + x * LANES, LANES)
    collect(ROWZ)
    o_gt[:, pl.ds(ocol, LANES)] = dot_tn(pickt[...], zr[...].reshape(640, LANES)).astype(BF16)
    x_spread(TAB, column(x, c), column, columns)

    collect(GWZ)
    gsum = gzr[0]
    for i in range(1, NZ):
        gsum = gsum + gzr[i]
    gsum = gsum * (1.0 / 256.0)
    for i in range(G):
        gxs[i] = jnp.where(row8 == 0, gsum[i : i + 1], gsum[8 + i : 9 + i])
    gxr[m] = gxs[m]
    spread(GWX, m, gpeer, lambda i: gxs.at[i], lambda i: gxr.at[i], gxr.at[pl.ds(0, 7)])

    collect(GIX)
    collect(EDGE)
    gix[x] = jnp.zeros((ROWS, C), BF16)
    total = pb[2 * x + c]
    edge = ed[0, 0:1]
    for i in range(NX):
        total = total + gix[i].astype(F32)
        if i:
            edge = edge + ed[i, 0:1]
    edge = jnp.where(s != c * 63, edge, 0.0)
    total = total + jnp.where(iota((ROWS, C), 0) == c * 127, edge, 0.0)
    o_gi[0] = total.astype(BF16)

    x_hand_on(TAB, column, columns)
    collect(GWX)
    for i in range(G):
        qi, ci = i // 2, i % 2
        taps = (1, 3) if ci == 0 else (2, 0)
        for t, k in enumerate(taps):
            o_gw[:, k * C + qi * LANES : k * C + (qi + 1) * LANES] = gxr[i, t : t + 1]
    collect(TAB)
    collect(TAB + 4)

    for finish in pending:
        finish()


def place(gi, gw, gt, o_gi, o_gw, o_gt, sem):
    copies = [pltpu.make_async_copy(a, b, sem.at[k]) for k, (a, b) in enumerate(((gt, o_gt), (gi, o_gi), (gw, o_gw)))]
    for copy in copies:
        copy.start()
    for copy in copies:
        copy.wait()


def body(inputs, weight, table, grad_out, clip_speaker, part_speaker, quote_bounds):
    vmem = pl.BlockSpec(memory_space=pltpu.VMEM)
    hbm = pl.BlockSpec(memory_space=pltpu.HBM)
    smem = pl.BlockSpec(memory_space=pltpu.SMEM)
    V = pltpu.VMEM
    large = [pltpu.with_memory_space_constraint(a, pltpu.HBM) for a in (inputs, weight, table, grad_out, quote_bounds)]
    outs = pl.pallas_call(
        kernel,
        out_shape=(
            jax.ShapeDtypeStruct(inputs.shape, BF16),
            jax.ShapeDtypeStruct(weight.shape, F32),
            jax.ShapeDtypeStruct(table.shape, BF16),
        ),
        in_specs=[hbm] * 4 + [smem] * 2 + [hbm],
        out_specs=(vmem, vmem, vmem),
        scratch_shapes=[
            V((1, 4 * C), BF16),
            pltpu.SMEM((1, 1, 2), jnp.int32),
            V((G, 8, LANES), F32),
            V((G, 8, LANES), F32),
            V((NZ, 8, LANES), F32),
            V((NY, 8, LANES), F32),
            V((NY, NZ, 16, LANES), BF16),
            V((C, 2 * LANES), BF16),
            V((NZ, 16, 2 * LANES), BF16),
            V((NZ, 16, 2 * LANES), BF16),
            V((16, 2 * LANES), F32),
            V((G, ROWS, C), BF16),
            V((NX, 16, C), BF16),
            V((G * ROWS, 2 * C), BF16),
            V((2 * ROWS, C), BF16),
            V((G, ROWS, LANES), BF16),
            V((G, ROWS, LANES), BF16),
            V((2 * C, 2 * C), BF16),
            V((2 * C, LANES), BF16),
            V((640, C), BF16),
            V((G * ROWS, LANES), BF16),
            V((2, 16, LANES), F32),
            V((16, LANES), F32),
            V((NY, 16, LANES), F32),
            V((NZ, 80, LANES), BF16),
            V((NY, LANES, LANES), BF16),
            V((NY, LANES, LANES), BF16),
            V((NZ, 16, LANES), F32),
            V((NZ, 16, LANES), F32),
            V((G, 8, LANES), F32),
            V((G, 8, LANES), F32),
            V((G, ROWS, C), F32),
            V((NX, ROWS, C), BF16),
            V((NX, ROWS, C), BF16),
            V((NX, ROWS, C), BF16),
            V((NX, ROWS, C), BF16),
            V((NX, 8, C), F32),
            V((NX, 8, C), F32),
            pltpu.SemaphoreType.DMA((CHANNELS,)),
            pltpu.SemaphoreType.DMA((CHANNELS,)),
            pltpu.SemaphoreType.DMA((6,)),
        ],
        compiler_params=pltpu.CompilerParams(
            collective_id=0, has_side_effects=True, vmem_limit_bytes=48 * 1024 * 1024
        ),
        cost_estimate=pl.CostEstimate(flops=2_000_000_000, bytes_accessed=8_000_000, transcendentals=131072),
    )(*large[:4], clip_speaker, part_speaker, large[4])
    return pl.pallas_call(
        place,
        out_shape=[jax.ShapeDtypeStruct(o.shape, o.dtype) for o in outs],
        in_specs=[pl.BlockSpec(memory_space=pl.ANY)] * 3,
        out_specs=[hbm] * 3,
        scratch_shapes=[pltpu.SemaphoreType.DMA((3,))],
        compiler_params=pltpu.CompilerParams(vmem_limit_bytes=4 * 1024 * 1024),
    )(*outs)


def solution(mesh):
    placed = (
        P("dp", "seq", None),
        P(("dp", "seq"), None),
        P("dp", None),
        P("dp", "seq", None),
        P("dp"),
        P("dp", "seq"),
        P("dp", "seq", None),
    )
    return jax.shard_map(
        body,
        mesh=mesh,
        in_specs=placed,
        out_specs=(P("dp", "seq", None), P(("dp", "seq"), None), P("dp", None)),
        check_vma=False,
    )
```
